32 devices in a mesh: row: 4 (over y, x), col: 8 (over z, core).
Axes of the slice: x: 2, y: 2, z: 4, core: 2. Of those that a mesh axis runs over, the one named last changes fastest.
Arguments:
- attributes: bfloat16 [16384, 128], P(('row', 'col')), may hold values from -6 to 6
- adj_values: bfloat16 [4, 8, 192, 128, 128], P('row', 'col'), may hold values from 0 to 3, as said below
- adj_rows: int32 [4, 8, 192], P('row', 'col'), may hold values from 0 to 31
- adj_cols: int32 [4, 8, 192], P('row', 'col'), may hold values from 0 to 15
- adj_count: int32 [4, 8], P('row', 'col'), may hold values from 1 to 192, as said below
- pair_ids: int32 [128, 4], P(('row', 'col')), may hold values from 0 to 15
- struct_target: bfloat16 [16384, 4, 128], P(('row', 'col')), may hold values from 0 to 1
- w_first: bfloat16 [128, 512], replicated, may hold values from -0.5 to 0.5
- w_rest: bfloat16 [1, 256, 512], replicated, may hold values from -0.375 to 0.375
- layer_bias: float32 [1, 256], replicated, may hold values from -3 to 3
- w_attr: bfloat16 [256, 128], replicated, may hold values from -0.375 to 0.375
- attr_bias: float32 [128], replicated, may hold values from -3 to 3
Outputs:
- anomaly: float32 [16384], P(('row', 'col'))
The draws below stay inside these ranges and needn't reach their ends.
Inputs may be any that keep to these rules, and one draw needn't show every extreme that they name: `adj_count`: every tile has at least one live slot, and some tile has all 192 live in every draw. `adj_values`: nonnegative entries; slots at or past a tile's count are ignored.
All inputs are finite; a program needn't handle non-finite values.
Results may differ from the reference program's by a relative error of at most 0.00075.
Values may be sent and summed in bfloat16 or wider, within the bound.
A program may use at most 128 MiB of HBM per device.

```python
import math
import jax
import jax.numpy as jnp
from jax import lax

F_IN = 128
HID = 256
BLK = 128
LAYERS = 2
PAIRS = 4
V_DEV = 512
NODES = 16384
BLOCKS_DEV = 4
NODE_BLOCKS = 128
TILE_ROWB = 32
TILE_COLB = 16
K_CAP = 192
N_ROW = 4
N_COL = 8


def draw_adj_values(key, part):
    key = jax.random.fold_in(key, 11)
    key_main = jax.random.fold_in(key, 1)
    col_ramp = 1.0 + 2.0 * jnp.arange(N_COL, dtype=jnp.float32) / max(N_COL - 1, 1)
    uniform_part = jax.random.uniform(key_main, (N_ROW, N_COL, K_CAP, BLK, BLK), jnp.float32)
    return (uniform_part * col_ramp[None, :, None, None, None]).astype(jnp.bfloat16)


def draw_adj_count(key, part):
    key = jax.random.fold_in(key, 23)
    key_shift = jax.random.fold_in(key, 1)
    key_jitter = jax.random.fold_in(key, 2)
    key_spot = jax.random.fold_in(key, 3)
    shifts = jax.random.randint(key_shift, (N_ROW, N_COL), 0, 3)
    base_counts = K_CAP // jnp.power(jnp.int32(2), shifts.astype(jnp.int32))
    jitter = jax.random.randint(key_jitter, (N_ROW, N_COL), 0, K_CAP // 8 + 1)
    counts = jnp.maximum(base_counts - jitter, 1).astype(jnp.int32)
    spot = jax.random.randint(key_spot, (), 0, N_ROW * N_COL)
    flattened = counts.reshape(-1).at[spot].set(K_CAP)
    return flattened.reshape(N_ROW, N_COL).astype(jnp.int32)


def plant(entries, own_key, least, top_value):
    longest = entries.shape.index(max(entries.shape))
    spots = []
    for shift in (0, 1):
        where = [jax.random.randint(jax.random.fold_in(own_key, axis), (), 0, length) for axis, length in enumerate(entries.shape)]
        where[longest] = (where[longest] + shift) % entries.shape[longest]
        spots.append(tuple(where))
    return entries.at[spots[0]].set(least).at[spots[1]].set(top_value)


def block_scale(rng, extent, cuts, smallest, largest):
    def one(axis_at, blocks):
        heights = jax.random.uniform(jax.random.fold_in(jax.random.fold_in(rng, 6), axis_at), (blocks,), jnp.float32, smallest / len(cuts), largest / len(cuts))
        return jnp.repeat(jnp.exp(heights), extent[axis_at] // blocks).reshape((-1,) + (1,) * (len(extent) - axis_at - 1))

    level = one(*cuts[0])
    for cut in cuts[1:]:
        level = level * one(*cut)
    return level


def centred(stream_key, shape, deviation, most, cuts=(), kind=jnp.bfloat16):
    values = deviation * jax.random.normal(stream_key, shape, jnp.float32)
    if cuts:
        values = values * block_scale(stream_key, shape, cuts, -0.22, 0.18)
    return jnp.clip(values, -most, most).astype(kind)


def setup_inputs(seed: int = 0) -> dict:
    splits = jax.random.split(jax.random.key(seed), 13)
    attributes = centred(splits[0], (NODES, F_IN), 1.0, 6.0, ((0, 32),))
    adj_values = draw_adj_values(jax.random.fold_in(splits[12], 71), 0)
    adj_rows = plant(jax.random.randint(splits[2], (N_ROW, N_COL, K_CAP), 0, TILE_ROWB), jax.random.fold_in(splits[2], 1), 0, TILE_ROWB - 1).astype(jnp.int32)
    adj_cols = plant(jax.random.randint(splits[3], (N_ROW, N_COL, K_CAP), 0, TILE_COLB), jax.random.fold_in(splits[3], 1), 0, TILE_COLB - 1).astype(jnp.int32)
    adj_count = draw_adj_count(jax.random.fold_in(splits[12], 71), 0)
    pair_ids = plant(jax.random.randint(splits[5], (NODE_BLOCKS, PAIRS), 0, TILE_COLB), jax.random.fold_in(splits[5], 1), 0, TILE_COLB - 1).astype(jnp.int32)
    struct_target = jnp.clip(1.0 * jax.random.uniform(splits[6], (NODES, PAIRS, BLK), jnp.float32) ** block_scale(splits[6], (NODES, PAIRS, BLK), ((0, 32),), -0.2, 0.2), 0.0, 1.0).astype(jnp.bfloat16)
    w_first = centred(splits[7], (F_IN, 2 * HID), F_IN ** -0.5, 0.5)
    w_rest = centred(splits[8], (LAYERS - 1, HID, 2 * HID), HID ** -0.5, 0.375)
    layer_bias = centred(splits[9], (LAYERS - 1, HID), 0.5, 3.0, (), jnp.float32)
    w_attr = centred(splits[10], (HID, F_IN), HID ** -0.5, 0.375)
    attr_bias = centred(splits[11], (F_IN,), 0.5, 3.0, (), jnp.float32)
    return {"attributes": attributes, "adj_values": adj_values, "adj_rows": adj_rows, "adj_cols": adj_cols, "adj_count": adj_count, "pair_ids": pair_ids, "struct_target": struct_target, "w_first": w_first, "w_rest": w_rest, "layer_bias": layer_bias, "w_attr": w_attr, "attr_bias": attr_bias}


epsilon = 1e-06
mix_alpha = 0.8

def tile_partial(panel_blocks, block_vals, row_ids, col_ids, live_mask):
    group_size = math.gcd(K_CAP, 32)
    num_groups = K_CAP // group_size

    def add_group(partial_sum, group_index):
        start = group_index * group_size
        vals_now = lax.dynamic_slice_in_dim(block_vals, start, group_size, 0).astype(jnp.float32)
        rows_now = lax.dynamic_slice_in_dim(row_ids, start, group_size, 0)
        cols_now = lax.dynamic_slice_in_dim(col_ids, start, group_size, 0)
        mask_now = lax.dynamic_slice_in_dim(live_mask, start, group_size, 0)
        picked = jnp.take(panel_blocks, cols_now, axis=0).astype(jnp.float32)
        products = jnp.einsum('gij,gjf->gif', vals_now, picked)
        return (partial_sum.at[rows_now].add(products * mask_now[:, None, None]), None)
    initial = jnp.zeros((TILE_ROWB, BLK, HID), jnp.float32)
    result, _ = lax.scan(add_group, initial, jnp.arange(num_groups, dtype=jnp.int32))
    return result

def aggregate(features, adj_values, adj_rows, adj_cols, live_all):
    grouped = features.reshape(N_ROW, N_COL, V_DEV, HID)

    def add_tile(total_sum, tile_index):
        row_index = tile_index // N_COL
        col_index = tile_index % N_COL
        column_group = lax.dynamic_index_in_dim(grouped, col_index, 1, False).reshape(TILE_COLB, BLK, HID)
        block_vals = lax.dynamic_index_in_dim(lax.dynamic_index_in_dim(adj_values, row_index, 0, False), col_index, 0, False)
        row_ids = lax.dynamic_index_in_dim(lax.dynamic_index_in_dim(adj_rows, row_index, 0, False), col_index, 0, False)
        col_ids = lax.dynamic_index_in_dim(lax.dynamic_index_in_dim(adj_cols, row_index, 0, False), col_index, 0, False)
        live_mask = lax.dynamic_index_in_dim(lax.dynamic_index_in_dim(live_all, row_index, 0, False), col_index, 0, False)
        partial_sum = tile_partial(column_group, block_vals, row_ids, col_ids, live_mask)
        current = lax.dynamic_index_in_dim(total_sum, row_index, 0, False)
        return (lax.dynamic_update_index_in_dim(total_sum, current + partial_sum, row_index, 0), None)
    initial = jnp.zeros((N_ROW, TILE_ROWB, BLK, HID), jnp.float32)
    total_sum, _ = lax.scan(add_tile, initial, jnp.arange(N_ROW * N_COL, dtype=jnp.int32))
    return total_sum.reshape(NODES, HID)

def reference(attributes, adj_values, adj_rows, adj_cols, adj_count, pair_ids, struct_target, w_first, w_rest, layer_bias, w_attr, attr_bias):
    slot_ids = jnp.arange(K_CAP, dtype=jnp.int32)
    live_all = (slot_ids[None, None, :] < adj_count[:, :, None]).astype(jnp.float32)
    row_mass = lax.optimization_barrier(jnp.sum(adj_values, axis=-1, dtype=jnp.float32)) * live_all[..., None]
    group_ids = jnp.broadcast_to(jnp.arange(N_ROW, dtype=jnp.int32)[:, None, None], adj_rows.shape)
    degree_terms = jnp.zeros((N_ROW, TILE_ROWB, BLK), jnp.float32).at[group_ids, adj_rows].add(row_mass)
    row_scale = lax.rsqrt(1.0 + degree_terms.reshape(NODES))
    hidden_state = attributes
    for layer_index in range(LAYERS):
        weight = w_first if layer_index == 0 else w_rest[layer_index - 1]
        projected = jnp.dot(hidden_state, weight, preferred_element_type=jnp.float32)
        features = projected[:, :HID].astype(jnp.bfloat16)
        summed = aggregate(features, adj_values, adj_rows, adj_cols, live_all)
        before = row_scale[:, None] * summed + projected[:, HID:]
        if layer_index > 0:
            before = before + layer_bias[layer_index - 1]
        hidden_state = jnp.tanh(before).astype(jnp.bfloat16)
    embedding = hidden_state
    rebuilt = jnp.dot(embedding, w_attr, preferred_element_type=jnp.float32) + attr_bias
    attr_error = jnp.sqrt(lax.optimization_barrier(jnp.mean((rebuilt - attributes.astype(jnp.float32)) ** 2, axis=1)) + epsilon)
    span_blocks = embedding.reshape(N_ROW * N_COL, BLOCKS_DEV, BLK, HID)
    all_blocks = embedding.reshape(NODE_BLOCKS, BLK, HID)
    span_pairs = pair_ids.reshape(N_ROW * N_COL, BLOCKS_DEV, PAIRS)
    span_target = struct_target.reshape(N_ROW * N_COL, V_DEV, PAIRS, BLK)

    def span_error(span_index):
        col_index = span_index % N_COL
        own_blocks = lax.dynamic_index_in_dim(span_blocks, span_index, 0, False).astype(jnp.float32)
        partner_ids = lax.dynamic_index_in_dim(span_pairs, span_index, 0, False)
        global_ids = (partner_ids // BLOCKS_DEV * N_COL + col_index) * BLOCKS_DEV + partner_ids % BLOCKS_DEV
        partners = jnp.take(all_blocks, global_ids.astype(jnp.int32), axis=0).astype(jnp.float32)
        logits = jnp.einsum('bif,bpjf->bipj', own_blocks, partners) * HID ** (-0.5)
        probability = jax.nn.sigmoid(logits).reshape(V_DEV, PAIRS, BLK)
        target = lax.dynamic_index_in_dim(span_target, span_index, 0, False).astype(jnp.float32)
        return jnp.sqrt(lax.optimization_barrier(jnp.mean((probability - target) ** 2, axis=(1, 2))) + epsilon)
    struct_error = lax.map(span_error, jnp.arange(N_ROW * N_COL, dtype=jnp.int32)).reshape(NODES)
    return mix_alpha * attr_error + (1.0 - mix_alpha) * struct_error
```

```python
import functools

import jax
import jax.numpy as jnp
from jax import lax
from jax.experimental import pallas as pl
from jax.experimental.pallas import tpu as pltpu
from jax.sharding import PartitionSpec as P

epsilon = 1e-06
mix_alpha = 0.8
MESH = pl.DeviceIdType.MESH
F32 = jnp.float32
BF16 = jnp.bfloat16
SUBS = 2
DEG_ROWS = 16


def dense_kernel(part_blocks, rows_ref, cols_ref, count_ref, vals_ref, out_ref):
    part = pl.program_id(0)
    blk = vals_ref.shape[1]
    out_ref[...] = jnp.zeros_like(out_ref)

    def add_slot(k, carry):
        row = rows_ref[k] - part * part_blocks

        @pl.when((row >= 0) & (row < part_blocks))
        def _():
            where_r = pl.ds(pl.multiple_of(row * blk, blk), blk)
            where_c = pl.ds(pl.multiple_of(cols_ref[k] * blk, blk), blk)
            out_ref[where_r, where_c] = out_ref[where_r, where_c] + vals_ref[k]

        return carry

    lax.fori_loop(0, count_ref[0], add_slot, 0)


def dense_tile(vals, row_ids, col_ids, count, row_blocks, col_blocks):
    cap, blk, _ = vals.shape
    part_blocks = 8
    grid_spec = pltpu.PrefetchScalarGridSpec(
        num_scalar_prefetch=3,
        grid=(row_blocks // part_blocks,),
        in_specs=[
            pl.BlockSpec((cap, blk, blk), lambda i, *_: (0, 0, 0), pipeline_mode=pl.Buffered(1))
        ],
        out_specs=pl.BlockSpec((part_blocks * blk, col_blocks * blk), lambda i, *_: (i, 0)),
    )
    return pl.pallas_call(
        functools.partial(dense_kernel, part_blocks),
        grid_spec=grid_spec,
        out_shape=jax.ShapeDtypeStruct((row_blocks * blk, col_blocks * blk), vals.dtype),
        compiler_params=pltpu.CompilerParams(vmem_limit_bytes=48 * 1024 * 1024),
        name="dense_tile",
    )(row_ids, col_ids, count, vals)


def graph_kernel(
    n_row,
    n_col,
    x_ref,
    a_ref,
    pair_ref,
    target_ref,
    w1_ref,
    w2_ref,
    b2_ref,
    wa_ref,
    ba_ref,
    out_ref,
    panel1,
    panel2,
    panel3,
    abuf,
    own1,
    own2,
    tot1,
    tot2,
    h1_ref,
    scale_ref,
    attr_ref,
    sib_out1,
    sib_in1,
    hop_out1,
    left_in1,
    right_in1,
    sib_out2,
    sib_in2,
    hop_out2,
    left_in2,
    right_in2,
    a_sem,
    g_send,
    g_recv,
    sib_send,
    sib_recv,
    hop_send,
    left_recv,
    right_recv,
):
    my_row = lax.axis_index("row")
    my_col = lax.axis_index("col")
    chips = n_col // 2
    chip = my_col // 2
    core = my_col % 2
    nodes, f_in = x_ref.shape
    hid = w2_ref.shape[0]
    blk = panel3.shape[1]
    sub = nodes // SUBS
    sub_blocks = sub // blk
    dev_blocks = nodes // blk
    steps = SUBS * chips

    sibling = (my_row, chip * 2 + 1 - core)
    right = (my_row, my_col + 2)
    left = (my_row, my_col - 2)
    peers = [(lax.rem(my_row + d, n_row), my_col) for d in range(1, n_row)]
    has_left = chip > 0
    has_right = chip < chips - 1

    far = jnp.maximum(chip, chips - 1 - chip)
    near = chips - 1 - far
    toward = jnp.where(2 * chip < chips - 1, 1, -1)

    def place(i):
        part = i // chips
        s = i - part * chips
        s2 = s - (far - near)
        paired = chip + (near - s2 // 2) * (1 - 2 * (s2 % 2))
        dest = jnp.where(s < far - near, chip + toward * (far - s), paired)
        return part, dest

    eye = lax.broadcasted_iota(jnp.int32, (blk, blk), 0) == lax.broadcasted_iota(
        jnp.int32, (blk, blk), 1
    )

    def to_row(square):
        return jnp.sum(jnp.where(eye, square, 0.0), axis=0, keepdims=True)

    def to_col(row):
        return jnp.sum(jnp.where(eye, jnp.broadcast_to(row, (blk, blk)), 0.0), axis=1, keepdims=True)

    def fetch(i, slot):
        part, dest = place(i)
        copies = []
        for which in range(2):
            pick = core if which == 0 else 1 - core
            start = pl.multiple_of((dest * 2 + pick) * nodes + part * sub, sub)
            copies.append(
                pltpu.make_async_copy(
                    a_ref.at[pl.ds(start, sub), :], abuf.at[slot, which], a_sem.at[slot, which]
                )
            )
        return copies

    def remote(src, dst, send, recv, device):
        return pltpu.make_async_remote_copy(
            src_ref=src,
            dst_ref=dst,
            send_sem=send,
            recv_sem=recv,
            device_id=device,
            device_id_type=MESH,
        )

    for copy in fetch(0, 0):
        copy.start()

    barrier = pltpu.get_barrier_semaphore()
    for device in [sibling] + peers:
        pl.semaphore_signal(barrier, inc=1, device_id=device, device_id_type=MESH)

    @pl.when(has_left)
    def _():
        pl.semaphore_signal(barrier, inc=1, device_id=left, device_id_type=MESH)

    @pl.when(has_right)
    def _():
        pl.semaphore_signal(barrier, inc=1, device_id=right, device_id_type=MESH)

    panel1[:, :, f_in:] = jnp.ones((n_row, nodes, panel1.shape[2] - f_in), BF16)
    panel1[my_row, :, :f_in] = x_ref[...]

    pl.semaphore_wait(barrier, n_row + jnp.minimum(chip, 1) + jnp.minimum(chips - 1 - chip, 1))

    def part1(row, part):
        return panel1.at[row, pl.ds(part * sub, sub), pl.ds(0, f_in)]

    def part2(row, part):
        return panel2.at[row, pl.ds(part * sub, sub), :]

    def part3(row, part):
        return panel3.at[pl.ds(row * dev_blocks + part * sub_blocks, sub_blocks)]

    def share(stage, view, part):
        for d in range(1, n_row):
            remote(
                view(my_row, part),
                view(my_row, part),
                g_send.at[stage, d - 1, part],
                g_recv.at[stage, d - 1, part],
                peers[d - 1],
            ).start()

    def gathered(stage, view, sent):
        for part in range(SUBS):
            for d in range(1, n_row):
                source = lax.rem(my_row + n_row - d, n_row)
                copy = remote(
                    view(my_row if sent else source, part),
                    view(my_row if sent else source, part),
                    g_send.at[stage, d - 1, part],
                    g_recv.at[stage, d - 1, part],
                    peers[d - 1],
                )
                if sent:
                    copy.wait_send()
                else:
                    copy.wait_recv()

    for part in range(SUBS):
        share(0, part1, part)
    gathered(0, part1, False)

    def aggregate(layer, panel, own, tot, sib_out, sib_in, hop_out, left_in, right_in, finish):
        def product(slot, which):
            total = None
            for r in range(n_row):
                term = jnp.dot(
                    abuf[slot, which, :, r * nodes : (r + 1) * nodes],
                    panel[r],
                    preferred_element_type=F32,
                )
                total = term if total is None else total + term
            return total

        def store(dst, value):
            if layer == 1:
                dst[...] = value.astype(dst.dtype)
                return
            dst[:sub, :] = value[:, :f_in].astype(dst.dtype)
            lane = lax.broadcasted_iota(jnp.int32, (DEG_ROWS, blk), 0)
            degree = jnp.zeros((DEG_ROWS, blk), F32)
            for b in range(sub_blocks):
                row = to_row(value[b * blk : (b + 1) * blk, f_in : f_in + blk])
                degree = jnp.where(lane == b, jnp.broadcast_to(row, (DEG_ROWS, blk)), degree)
            dst[sub:, :] = degree.astype(dst.dtype)

        def sib_copy(at):
            return remote(
                sib_out.at[at], sib_in.at[at], sib_send.at[layer, at], sib_recv.at[layer, at], sibling
            )

        def right_copy(at, device):
            return remote(
                hop_out.at[at], left_in.at[at], hop_send.at[layer, at], left_recv.at[layer, at], device
            )

        def left_copy(at, device):
            return remote(
                hop_out.at[at], right_in.at[at], hop_send.at[layer, at], right_recv.at[layer, at], device
            )

        def body(i, carry):
            @pl.when(i < steps)
            def _():
                slot = i % 2

                @pl.when(i + 1 < steps)
                def _():
                    for copy in fetch(i + 1, (i + 1) % 2):
                        copy.start()

                for copy in fetch(i, slot):
                    copy.wait()
                part, dest = place(i)
                at = part * chips + dest
                store(sib_out.at[at], product(slot, 1))
                sib_copy(at).start()
                store(own.at[slot], product(slot, 0))

            @pl.when(i >= 1)
            def _():
                j = i - 1
                part, dest = place(j)
                at = part * chips + dest
                sib_copy(at).wait_recv()
                tot[...] = own[j % 2] + sib_in[at].astype(F32)

                @pl.when((dest >= chip) & has_left)
                def _():
                    right_copy(at, sibling).wait_recv()
                    tot[...] += left_in[at].astype(F32)

                @pl.when((dest <= chip) & has_right)
                def _():
                    left_copy(at, sibling).wait_recv()
                    tot[...] += right_in[at].astype(F32)

                @pl.when(dest > chip)
                def _():
                    hop_out[at] = tot[...].astype(BF16)
                    right_copy(at, right).start()

                @pl.when(dest < chip)
                def _():
                    hop_out[at] = tot[...].astype(BF16)
                    left_copy(at, left).start()

                @pl.when(dest == chip)
                def _():
                    finish(part)

            return carry

        lax.fori_loop(0, steps + 1, body, 0)

        def drain():
            def one(i, carry):
                part, dest = place(i)
                at = part * chips + dest
                sib_copy(at).wait_send()

                @pl.when(dest != chip)
                def _():
                    right_copy(at, sibling).wait_send()

                return carry

            lax.fori_loop(0, steps, one, 0)

        return drain

    def finish1(part):
        for b in range(sub_blocks):
            rows = pl.ds(pl.multiple_of(part * sub + b * blk, blk), blk)
            scale = lax.rsqrt(1.0 + to_col(tot1[sub + b : sub + b + 1, :]))
            scale_ref[rows, :] = jnp.broadcast_to(scale, (blk, blk))
            mean = tot1[b * blk : (b + 1) * blk, :] * scale
            high = mean.astype(BF16)
            low = (mean - high.astype(F32)).astype(BF16)
            before = jnp.dot(high, w1_ref[:, :hid], preferred_element_type=F32)
            before += jnp.dot(low, w1_ref[:, :hid], preferred_element_type=F32)
            before += jnp.dot(x_ref[rows, :], w1_ref[:, hid:], preferred_element_type=F32)
            hidden = jnp.tanh(before).astype(BF16)
            h1_ref[rows, :] = hidden
            panel2[my_row, rows, :] = jnp.dot(
                hidden, w2_ref[:, :hid], preferred_element_type=F32
            ).astype(BF16)
        share(1, part2, part)

    drain1 = aggregate(
        0, panel1, own1, tot1, sib_out1, sib_in1, hop_out1, left_in1, right_in1, finish1
    )
    for copy in fetch(0, 0):
        copy.start()
    gathered(1, part2, False)

    def finish2(part):
        for b in range(sub_blocks):
            rows = pl.ds(pl.multiple_of(part * sub + b * blk, blk), blk)
            before = jnp.dot(h1_ref[rows, :], w2_ref[:, hid:], preferred_element_type=F32)
            before += tot2[b * blk : (b + 1) * blk, :] * scale_ref[rows, 0:1] + b2_ref[...]
            panel3[my_row * dev_blocks + part * sub_blocks + b] = jnp.tanh(before).astype(BF16)
        share(2, part3, part)

    drain2 = aggregate(
        1, panel2, own2, tot2, sib_out2, sib_in2, hop_out2, left_in2, right_in2, finish2
    )

    def attr_block(b, carry):
        rows = pl.ds(pl.multiple_of(b * blk, blk), blk)
        rebuilt = jnp.dot(
            panel3[my_row * dev_blocks + b], wa_ref[...], preferred_element_type=F32
        )
        diff = rebuilt + ba_ref[...] - x_ref[rows, :].astype(F32)
        error = jnp.sqrt(jnp.mean(diff * diff, axis=1, keepdims=True) + epsilon)
        attr_ref[rows, :] = jnp.broadcast_to(error, (blk, blk))
        return carry

    lax.fori_loop(0, dev_blocks, attr_block, 0)
    drain1()
    drain2()
    for stage, view in enumerate((part1, part2, part3)):
        gathered(stage, view, True)
    gathered(2, part3, False)

    pair_count = pair_ref.shape[1]

    def decode(b, carry):
        rows = pl.ds(pl.multiple_of(b * blk, blk), blk)
        mine = panel3[my_row * dev_blocks + b]
        total = jnp.zeros((blk, blk), F32)
        for j in range(pair_count):
            logits = lax.dot_general(
                mine,
                panel3[pair_ref[b, j]],
                (((1,), (1,)), ((), ())),
                preferred_element_type=F32,
            ) * hid ** (-0.5)
            diff = jax.nn.sigmoid(logits) - target_ref[rows, j * blk : (j + 1) * blk].astype(F32)
            total += diff * diff
        mean = jnp.sum(total, axis=1, keepdims=True) * (1.0 / (pair_count * blk))
        score = mix_alpha * attr_ref[rows, :] + (1.0 - mix_alpha) * jnp.sqrt(mean + epsilon)
        out_ref[pl.ds(b, 1), :] = to_row(score)
        return carry

    lax.fori_loop(0, dev_blocks, decode, 0)


def per_device(
    attributes,
    adj_values,
    adj_rows,
    adj_cols,
    adj_count,
    pair_ids,
    struct_target,
    w_first,
    w_rest,
    layer_bias,
    w_attr,
    attr_bias,
):
    n_row = lax.axis_size("row")
    n_col = lax.axis_size("col")
    nodes, f_in = attributes.shape
    blk = adj_values.shape[3]
    hid = w_rest.shape[1]
    row_blocks = n_col * nodes // blk
    col_blocks = n_row * nodes // blk
    dense = dense_tile(
        adj_values[0, 0], adj_rows[0, 0], adj_cols[0, 0], adj_count[0], row_blocks, col_blocks
    )
    sub = nodes // SUBS
    steps = SUBS * (n_col // 2)
    wide = 2 * blk
    vmem = pl.BlockSpec(memory_space=pltpu.VMEM)
    ring1 = pltpu.VMEM((steps, sub + DEG_ROWS, f_in), BF16)
    ring2 = pltpu.VMEM((steps, sub, hid), BF16)
    scores = pl.pallas_call(
        functools.partial(graph_kernel, n_row, n_col),
        out_shape=jax.ShapeDtypeStruct((nodes // blk, blk), F32),
        in_specs=[
            vmem,
            pl.BlockSpec(memory_space=pl.ANY),
            pl.BlockSpec(memory_space=pltpu.SMEM),
        ]
        + [vmem] * 6,
        out_specs=vmem,
        scratch_shapes=[
            pltpu.VMEM((n_row, nodes, f_in + blk), BF16),
            pltpu.VMEM((n_row, nodes, hid), BF16),
            pltpu.VMEM((col_blocks, blk, hid), BF16),
            pltpu.VMEM((2, 2, sub, col_blocks * blk), BF16),
            pltpu.VMEM((2, sub + DEG_ROWS, f_in), F32),
            pltpu.VMEM((2, sub, hid), F32),
            pltpu.VMEM((sub + DEG_ROWS, f_in), F32),
            pltpu.VMEM((sub, hid), F32),
            pltpu.VMEM((nodes, hid), BF16),
            pltpu.VMEM((nodes, blk), F32),
            pltpu.VMEM((nodes, blk), F32),
        ]
        + [ring1] * 5
        + [ring2] * 5
        + [
            pltpu.SemaphoreType.DMA((2, 2)),
            pltpu.SemaphoreType.DMA((3, n_row - 1, SUBS)),
            pltpu.SemaphoreType.DMA((3, n_row - 1, SUBS)),
            pltpu.SemaphoreType.DMA((2, steps)),
            pltpu.SemaphoreType.DMA((2, steps)),
            pltpu.SemaphoreType.DMA((2, steps)),
            pltpu.SemaphoreType.DMA((2, steps)),
            pltpu.SemaphoreType.DMA((2, steps)),
        ],
        compiler_params=pltpu.CompilerParams(
            collective_id=0, has_side_effects=True, vmem_limit_bytes=56 * 1024 * 1024
        ),
        name="graph_layers",
    )(
        attributes,
        dense,
        pair_ids,
        struct_target.reshape(nodes, -1),
        w_first,
        w_rest[0],
        layer_bias,
        w_attr,
        attr_bias.reshape(1, -1),
    )
    return scores.reshape(nodes)


def solution(mesh):
    return jax.shard_map(
        per_device,
        mesh=mesh,
        in_specs=(
            P(("row", "col"), None),
            P("row", "col", None, None, None),
            P("row", "col", None),
            P("row", "col", None),
            P("row", "col"),
            P(("row", "col"), None),
            P(("row", "col"), None, None),
            P(),
            P(),
            P(),
            P(),
            P(),
        ),
        out_specs=P(("row", "col")),
        check_vma=False,
    )
```

```python
import functools

import jax
import jax.numpy as jnp
from jax import lax
from jax.experimental import pallas as pl
from jax.experimental.pallas import tpu as pltpu
from jax.sharding import PartitionSpec as P

epsilon = 1e-06
mix_alpha = 0.8
MESH = pl.DeviceIdType.MESH
F32 = jnp.float32
BF16 = jnp.bfloat16
SUBS = 4
LAG = 2
DEG_ROWS = 16


def dense_kernel(part_blocks, rows_ref, cols_ref, count_ref, vals_hbm, out_ref, vals_ref, lists, sizes, sem):
    part = pl.program_id(0)
    blk = vals_ref.shape[1]
    load = pltpu.make_async_copy(vals_hbm, vals_ref, sem)

    @pl.when(part == 0)
    def _():
        load.start()
        for q in range(sizes.shape[0]):
            sizes[q] = 0

        def assign(k, carry):
            q = lax.div(rows_ref[k], part_blocks)
            n = sizes[q]
            lists[q, n] = k
            sizes[q] = n + 1
            return carry

        lax.fori_loop(0, count_ref[0], assign, 0)

    out_ref[...] = jnp.zeros_like(out_ref)

    @pl.when(part == 0)
    def _():
        load.wait()

    def add_slot(n, carry):
        k = lists[part, n]
        row = rows_ref[k] - part * part_blocks
        where_r = pl.ds(pl.multiple_of(row * blk, blk), blk)
        where_c = pl.ds(pl.multiple_of(cols_ref[k] * blk, blk), blk)
        out_ref[where_r, where_c] = out_ref[where_r, where_c] + vals_ref[k]
        return carry

    lax.fori_loop(0, sizes[part], add_slot, 0)


def dense_tile(vals, row_ids, col_ids, count, row_blocks, col_blocks):
    cap, blk, _ = vals.shape
    part_blocks = 4
    parts = row_blocks // part_blocks
    grid_spec = pltpu.PrefetchScalarGridSpec(
        num_scalar_prefetch=3,
        grid=(parts,),
        in_specs=[pl.BlockSpec(memory_space=pl.ANY)],
        out_specs=pl.BlockSpec((part_blocks * blk, col_blocks * blk), lambda i, *_: (i, 0)),
        scratch_shapes=[
            pltpu.VMEM((cap, blk, blk), vals.dtype),
            pltpu.SMEM((parts, cap), jnp.int32),
            pltpu.SMEM((parts,), jnp.int32),
            pltpu.SemaphoreType.DMA,
        ],
    )
    dense_bytes = row_blocks * col_blocks * blk * blk * 2
    return pl.pallas_call(
        functools.partial(dense_kernel, part_blocks),
        grid_spec=grid_spec,
        out_shape=jax.ShapeDtypeStruct((row_blocks * blk, col_blocks * blk), vals.dtype),
        compiler_params=pltpu.CompilerParams(vmem_limit_bytes=48 * 1024 * 1024),
        cost_estimate=pl.CostEstimate(
            flops=dense_bytes, bytes_accessed=2 * dense_bytes, transcendentals=0
        ),
        name="dense_tile",
    )(row_ids, col_ids, count, vals)


def graph_kernel(
    n_row,
    n_col,
    *refs,
):
    x_refs, refs = refs[:n_row], refs[n_row:]
    x_ref = x_refs[0]
    (
    a_ref,
    pair_ref,
    target_ref,
    w1_ref,
    w2_ref,
    b2_ref,
    wa_ref,
    ba_ref,
    out_ref,
    panel1,
    panel2,
    panel3,
    abuf,
    own1,
    own2,
    tot1,
    tot2,
    h1_ref,
    scale_ref,
    attr_ref,
    sib_out1,
    sib_in1,
    hop_out1,
    left_in1,
    right_in1,
    sib_out2,
    sib_in2,
    hop_out2,
    left_in2,
    right_in2,
    a_sem,
    g_send,
    g_recv,
    sib_send,
    sib_recv,
    hop_send,
    left_recv,
    right_recv,
    ) = refs
    my_row = lax.axis_index("row")
    my_col = lax.axis_index("col")
    chips = n_col // 2
    chip = my_col // 2
    core = my_col % 2
    nodes, f_in = x_ref.shape
    hid = w2_ref.shape[0]
    blk = panel3.shape[1]
    sub = nodes // SUBS
    sub_blocks = sub // blk
    dev_blocks = nodes // blk
    steps = SUBS * chips

    sibling = (my_row, chip * 2 + 1 - core)
    right = (my_row, my_col + 2)
    left = (my_row, my_col - 2)
    peers = [(lax.rem(my_row + d, n_row), my_col) for d in range(1, n_row)]
    has_left = chip > 0
    has_right = chip < chips - 1

    far = jnp.maximum(chip, chips - 1 - chip)
    near = chips - 1 - far
    toward = jnp.where(2 * chip < chips - 1, 1, -1)

    def place(i):
        r = i % chips
        later = (r == chips - 1) & (i < steps - 1)
        earlier = (r == 0) & (i > 0)
        i = i + jnp.where(later, 1, 0) - jnp.where(earlier, 1, 0)
        part = i // chips
        s = i - part * chips
        s2 = s - (far - near)
        paired = chip + (near - s2 // 2) * (1 - 2 * (s2 % 2))
        dest = jnp.where(s < far - near, chip + toward * (far - s), paired)
        return part, dest

    eye = lax.broadcasted_iota(jnp.int32, (blk, blk), 0) == lax.broadcasted_iota(
        jnp.int32, (blk, blk), 1
    )

    def to_row(square):
        return jnp.sum(jnp.where(eye, square, 0.0), axis=0, keepdims=True)

    def to_col(row):
        return jnp.sum(jnp.where(eye, jnp.broadcast_to(row, (blk, blk)), 0.0), axis=1, keepdims=True)

    def fetch(i, slot):
        part, dest = place(i)
        copies = []
        for which in range(2):
            pick = core if which == 0 else 1 - core
            start = pl.multiple_of((dest * 2 + pick) * nodes + part * sub, sub)
            copies.append(
                pltpu.make_async_copy(
                    a_ref.at[pl.ds(start, sub), :],
                    abuf.at[slot, pl.ds(which * sub, sub), :],
                    a_sem.at[slot, which],
                )
            )
        return copies

    def remote(src, dst, send, recv, device):
        return pltpu.make_async_remote_copy(
            src_ref=src,
            dst_ref=dst,
            send_sem=send,
            recv_sem=recv,
            device_id=device,
            device_id_type=MESH,
        )

    for copy in fetch(0, 0):
        copy.start()

    barrier = pltpu.get_barrier_semaphore()
    for device in [sibling] + peers:
        pl.semaphore_signal(barrier, inc=1, device_id=device, device_id_type=MESH)

    @pl.when(has_left)
    def _():
        pl.semaphore_signal(barrier, inc=1, device_id=left, device_id_type=MESH)

    @pl.when(has_right)
    def _():
        pl.semaphore_signal(barrier, inc=1, device_id=right, device_id_type=MESH)

    panel1[:, f_in:] = jnp.ones((n_row * nodes, panel1.shape[1] - f_in), BF16)
    for d in range(n_row):
        source = lax.rem(my_row + n_row - d, n_row)
        panel1[pl.ds(pl.multiple_of(source * nodes, nodes), nodes), :f_in] = x_refs[d][...]

    pl.semaphore_wait(barrier, n_row + jnp.minimum(chip, 1) + jnp.minimum(chips - 1 - chip, 1))

    def part2(row, part):
        return panel2.at[pl.ds(pl.multiple_of(row * nodes + part * sub, sub), sub), :]

    def part3(row, part):
        return panel3.at[pl.ds(row * dev_blocks + part * sub_blocks, sub_blocks)]

    def share(stage, view, part):
        for d in range(1, n_row):
            remote(
                view(my_row, part),
                view(my_row, part),
                g_send.at[stage, d - 1, part],
                g_recv.at[stage, d - 1, part],
                peers[d - 1],
            ).start()

    def gathered(stage, view, sent):
        for part in range(SUBS):
            for d in range(1, n_row):
                source = lax.rem(my_row + n_row - d, n_row)
                copy = remote(
                    view(my_row if sent else source, part),
                    view(my_row if sent else source, part),
                    g_send.at[stage, d - 1, part],
                    g_recv.at[stage, d - 1, part],
                    peers[d - 1],
                )
                if sent:
                    copy.wait_send()
                else:
                    copy.wait_recv()

    def aggregate(layer, panel, own, tot, sib_out, sib_in, hop_out, left_in, right_in, finish):
        def store(dst, value):
            if layer == 1:
                dst[...] = value.astype(dst.dtype)
                return
            dst[:sub, :] = value[:, :f_in].astype(dst.dtype)
            lane = lax.broadcasted_iota(jnp.int32, (DEG_ROWS, blk), 0)
            degree = jnp.zeros((DEG_ROWS, blk), F32)
            for b in range(sub_blocks):
                row = to_row(value[b * blk : (b + 1) * blk, f_in : f_in + blk])
                degree = jnp.where(lane == b, jnp.broadcast_to(row, (DEG_ROWS, blk)), degree)
            dst[sub:, :] = degree.astype(dst.dtype)

        def sib_copy(at):
            return remote(
                sib_out.at[at], sib_in.at[at], sib_send.at[layer, at], sib_recv.at[layer, at], sibling
            )

        def right_copy(at, device):
            return remote(
                hop_out.at[at], left_in.at[at], hop_send.at[layer, at], left_recv.at[layer, at], device
            )

        def left_copy(at, device):
            return remote(
                hop_out.at[at], right_in.at[at], hop_send.at[layer, at], right_recv.at[layer, at], device
            )

        def body(i, carry):
            @pl.when(i < steps)
            def _():
                slot = i % 2

                @pl.when(i + 1 < steps)
                def _():
                    for copy in fetch(i + 1, (i + 1) % 2):
                        copy.start()

                for copy in fetch(i, slot):
                    copy.wait()
                part, dest = place(i)
                at = part * chips + dest
                total = jnp.dot(abuf[slot], panel[...], preferred_element_type=F32)
                store(sib_out.at[at], total[sub:])
                sib_copy(at).start()
                store(own.at[i % (LAG + 1)], total[:sub])

            @pl.when(i >= LAG)
            def _():
                j = i - LAG
                part, dest = place(j)
                at = part * chips + dest
                sib_copy(at).wait_recv()
                tot[...] = own[j % (LAG + 1)] + sib_in[at].astype(F32)

                @pl.when((dest >= chip) & has_left)
                def _():
                    right_copy(at, sibling).wait_recv()
                    tot[...] += left_in[at].astype(F32)

                @pl.when((dest <= chip) & has_right)
                def _():
                    left_copy(at, sibling).wait_recv()
                    tot[...] += right_in[at].astype(F32)

                @pl.when(dest > chip)
                def _():
                    hop_out[at] = tot[...].astype(BF16)
                    right_copy(at, right).start()

                @pl.when(dest < chip)
                def _():
                    hop_out[at] = tot[...].astype(BF16)
                    left_copy(at, left).start()

                @pl.when(dest == chip)
                def _():
                    finish(part)

            return carry

        lax.fori_loop(0, steps + LAG, body, 0)

        def drain():
            def one(i, carry):
                part, dest = place(i)
                at = part * chips + dest
                sib_copy(at).wait_send()

                @pl.when(dest != chip)
                def _():
                    right_copy(at, sibling).wait_send()

                return carry

            lax.fori_loop(0, steps, one, 0)

        return drain

    def finish1(part):
        for b in range(sub_blocks):
            rows = pl.ds(pl.multiple_of(part * sub + b * blk, blk), blk)
            scale = lax.rsqrt(1.0 + to_col(tot1[sub + b : sub + b + 1, :]))
            scale_ref[rows, :] = jnp.broadcast_to(scale, (blk, blk))
            mean = tot1[b * blk : (b + 1) * blk, :] * scale
            high = mean.astype(BF16)
            low = (mean - high.astype(F32)).astype(BF16)
            before = jnp.dot(high, w1_ref[:, :hid], preferred_element_type=F32)
            before += jnp.dot(low, w1_ref[:, :hid], preferred_element_type=F32)
            before += jnp.dot(x_ref[rows, :], w1_ref[:, hid:], preferred_element_type=F32)
            hidden = jnp.tanh(before).astype(BF16)
            h1_ref[rows, :] = hidden
            mine = pl.ds(pl.multiple_of(my_row * nodes + part * sub + b * blk, blk), blk)
            panel2[mine, :] = jnp.dot(
                hidden, w2_ref[:, :hid], preferred_element_type=F32
            ).astype(BF16)
        share(0, part2, part)

    drain1 = aggregate(
        0, panel1, own1, tot1, sib_out1, sib_in1, hop_out1, left_in1, right_in1, finish1
    )
    for copy in fetch(0, 0):
        copy.start()
    gathered(0, part2, False)

    def finish2(part):
        for b in range(sub_blocks):
            rows = pl.ds(pl.multiple_of(part * sub + b * blk, blk), blk)
            before = jnp.dot(h1_ref[rows, :], w2_ref[:, hid:], preferred_element_type=F32)
            before += tot2[b * blk : (b + 1) * blk, :] * scale_ref[rows, 0:1] + b2_ref[...]
            panel3[my_row * dev_blocks + part * sub_blocks + b] = jnp.tanh(before).astype(BF16)
        share(1, part3, part)

    drain2 = aggregate(
        1, panel2, own2, tot2, sib_out2, sib_in2, hop_out2, left_in2, right_in2, finish2
    )

    def attr_block(b, carry):
        rows = pl.ds(pl.multiple_of(b * blk, blk), blk)
        rebuilt = jnp.dot(
            panel3[my_row * dev_blocks + b], wa_ref[...], preferred_element_type=F32
        )
        diff = rebuilt + ba_ref[...] - x_ref[rows, :].astype(F32)
        error = jnp.sqrt(jnp.mean(diff * diff, axis=1, keepdims=True) + epsilon)
        attr_ref[rows, :] = jnp.broadcast_to(error, (blk, blk))
        return carry

    lax.fori_loop(0, dev_blocks, attr_block, 0)
    drain1()
    drain2()
    for stage, view in enumerate((part2, part3)):
        gathered(stage, view, True)
    gathered(1, part3, False)

    pair_count = pair_ref.shape[1]

    def decode(b, carry):
        rows = pl.ds(pl.multiple_of(b * blk, blk), blk)
        mine = panel3[my_row * dev_blocks + b]
        total = jnp.zeros((blk, blk), F32)
        for j in range(pair_count):
            logits = lax.dot_general(
                mine,
                panel3[pair_ref[b, j]],
                (((1,), (1,)), ((), ())),
                preferred_element_type=F32,
            ) * hid ** (-0.5)
            diff = jax.nn.sigmoid(logits) - target_ref[rows, j, :].astype(F32)
            total += diff * diff
        mean = jnp.sum(total, axis=1, keepdims=True) * (1.0 / (pair_count * blk))
        score = mix_alpha * attr_ref[rows, :] + (1.0 - mix_alpha) * jnp.sqrt(mean + epsilon)
        out_ref[pl.ds(b, 1), :] = to_row(score)
        return carry

    lax.fori_loop(0, dev_blocks, decode, 0)


def per_device(
    attributes,
    adj_values,
    adj_rows,
    adj_cols,
    adj_count,
    pair_ids,
    struct_target,
    w_first,
    w_rest,
    layer_bias,
    w_attr,
    attr_bias,
):
    n_row = lax.axis_size("row")
    n_col = lax.axis_size("col")
    nodes, f_in = attributes.shape
    blk = adj_values.shape[3]
    hid = w_rest.shape[1]
    row_blocks = n_col * nodes // blk
    col_blocks = n_row * nodes // blk
    others = [
        lax.ppermute(attributes, "row", [(r, (r + d) % n_row) for r in range(n_row)])
        for d in range(1, n_row)
    ]
    dense = dense_tile(
        adj_values[0, 0], adj_rows[0, 0], adj_cols[0, 0], adj_count[0], row_blocks, col_blocks
    )
    sub = nodes // SUBS
    steps = SUBS * (n_col // 2)
    wide = 2 * blk
    vmem = pl.BlockSpec(memory_space=pltpu.VMEM)
    ring1 = pltpu.VMEM((steps, sub + DEG_ROWS, f_in), BF16)
    ring2 = pltpu.VMEM((steps, sub, hid), BF16)
    scores = pl.pallas_call(
        functools.partial(graph_kernel, n_row, n_col),
        out_shape=jax.ShapeDtypeStruct((nodes // blk, blk), F32),
        in_specs=[vmem] * n_row
        + [
            pl.BlockSpec(memory_space=pl.ANY),
            pl.BlockSpec(memory_space=pltpu.SMEM),
        ]
        + [vmem] * 6,
        out_specs=vmem,
        scratch_shapes=[
            pltpu.VMEM((n_row * nodes, f_in + blk), BF16),
            pltpu.VMEM((n_row * nodes, hid), BF16),
            pltpu.VMEM((col_blocks, blk, hid), BF16),
            pltpu.VMEM((2, 2 * sub, col_blocks * blk), BF16),
            pltpu.VMEM((LAG + 1, sub + DEG_ROWS, f_in), F32),
            pltpu.VMEM((LAG + 1, sub, hid), F32),
            pltpu.VMEM((sub + DEG_ROWS, f_in), F32),
            pltpu.VMEM((sub, hid), F32),
            pltpu.VMEM((nodes, hid), BF16),
            pltpu.VMEM((nodes, blk), F32),
            pltpu.VMEM((nodes, blk), F32),
        ]
        + [ring1] * 5
        + [ring2] * 5
        + [
            pltpu.SemaphoreType.DMA((2, 2)),
            pltpu.SemaphoreType.DMA((2, n_row - 1, SUBS)),
            pltpu.SemaphoreType.DMA((2, n_row - 1, SUBS)),
            pltpu.SemaphoreType.DMA((2, steps)),
            pltpu.SemaphoreType.DMA((2, steps)),
            pltpu.SemaphoreType.DMA((2, steps)),
            pltpu.SemaphoreType.DMA((2, steps)),
            pltpu.SemaphoreType.DMA((2, steps)),
        ],
        compiler_params=pltpu.CompilerParams(
            collective_id=0, has_side_effects=True, vmem_limit_bytes=56 * 1024 * 1024
        ),
        name="graph_layers",
    )(
        attributes,
        *others,
        dense,
        pair_ids,
        struct_target,
        w_first,
        w_rest[0],
        layer_bias,
        w_attr,
        attr_bias.reshape(1, -1),
    )
    return scores.reshape(nodes)


def solution(mesh):
    return jax.shard_map(
        per_device,
        mesh=mesh,
        in_specs=(
            P(("row", "col"), None),
            P("row", "col", None, None, None),
            P("row", "col", None),
            P("row", "col", None),
            P("row", "col"),
            P(("row", "col"), None),
            P(("row", "col"), None, None),
            P(),
            P(),
            P(),
            P(),
            P(),
        ),
        out_specs=P(("row", "col")),
        check_vma=False,
    )
```

```python
import functools

import jax
import jax.numpy as jnp
from jax import lax
from jax.experimental import pallas as pl
from jax.experimental.pallas import tpu as pltpu
from jax.sharding import PartitionSpec as P

epsilon = 1e-06
mix_alpha = 0.8
MESH = pl.DeviceIdType.MESH
F32 = jnp.float32
BF16 = jnp.bfloat16
SUBS = 2
GROUP = 2
DEG_ROWS = 16


def dense_kernel(part_blocks, rows_ref, cols_ref, count_ref, vals_hbm, out_ref, vals_ref, lists, sizes, sem):
    part = pl.program_id(0)
    blk = vals_ref.shape[1]
    load = pltpu.make_async_copy(vals_hbm, vals_ref, sem)

    @pl.when(part == 0)
    def _():
        load.start()
        for q in range(sizes.shape[0]):
            sizes[q] = 0

        def assign(k, carry):
            q = lax.div(rows_ref[0, 0, k], part_blocks)
            n = sizes[q]
            lists[q, n] = k
            sizes[q] = n + 1
            return carry

        lax.fori_loop(0, count_ref[0, 0], assign, 0)

    out_ref[...] = jnp.zeros_like(out_ref)

    @pl.when(part == 0)
    def _():
        load.wait()

    def add_slot(n, carry):
        k = lists[part, n]
        row = rows_ref[0, 0, k] - part * part_blocks
        where_r = pl.ds(pl.multiple_of(row * blk, blk), blk)
        where_c = pl.ds(pl.multiple_of(cols_ref[0, 0, k] * blk, blk), blk)
        out_ref[where_r, where_c] = out_ref[where_r, where_c] + vals_ref[k]
        return carry

    lax.fori_loop(0, sizes[part], add_slot, 0)


def dense_tile(vals, row_ids, col_ids, count, row_blocks, col_blocks):
    cap, blk, _ = vals.shape
    part_blocks = 4
    parts = row_blocks // part_blocks
    dense_bytes = row_blocks * col_blocks * blk * blk * 2
    return pl.pallas_call(
        functools.partial(dense_kernel, part_blocks),
        grid=(parts,),
        in_specs=[pl.BlockSpec(memory_space=pltpu.SMEM)] * 3
        + [pl.BlockSpec(memory_space=pl.ANY)],
        out_specs=pl.BlockSpec((part_blocks * blk, col_blocks * blk), lambda i: (i, 0)),
        scratch_shapes=[
            pltpu.VMEM((cap, blk, blk), vals.dtype),
            pltpu.SMEM((parts, cap), jnp.int32),
            pltpu.SMEM((parts,), jnp.int32),
            pltpu.SemaphoreType.DMA,
        ],
        out_shape=jax.ShapeDtypeStruct((row_blocks * blk, col_blocks * blk), vals.dtype),
        compiler_params=pltpu.CompilerParams(vmem_limit_bytes=48 * 1024 * 1024),
        cost_estimate=pl.CostEstimate(
            flops=dense_bytes, bytes_accessed=2 * dense_bytes, transcendentals=0
        ),
        name="dense_tile",
    )(row_ids, col_ids, count, vals)


def graph_kernel(
    n_row,
    n_col,
    x_ref,
    a_ref,
    pair_ref,
    target_ref,
    w1_ref,
    w2_ref,
    b2_ref,
    wa_ref,
    ba_ref,
    out_ref,
    panel1,
    panel2,
    panel3,
    abuf,
    own1,
    own2,
    tot1,
    tot2,
    h1_ref,
    scale_ref,
    attr_ref,
    sib_out1,
    sib_in1,
    hop_out1,
    left_in1,
    right_in1,
    sib_out2,
    sib_in2,
    hop_out2,
    left_in2,
    right_in2,
    a_sem,
    g_send,
    g_recv,
    sib_send,
    sib_recv,
    hop_send,
    left_recv,
    right_recv,
    prod,
):
    my_row = lax.axis_index("row")
    my_col = lax.axis_index("col")
    chips = n_col // 2
    chip = my_col // 2
    core = my_col % 2
    nodes, f_in = x_ref.shape
    hid = w2_ref.shape[0]
    blk = panel3.shape[1]
    sub = nodes // SUBS
    sub_blocks = sub // blk
    dev_blocks = nodes // blk
    steps = SUBS * chips

    sibling = (my_row, chip * 2 + 1 - core)
    right = (my_row, my_col + 2)
    left = (my_row, my_col - 2)
    peers = [(lax.rem(my_row + d, n_row), my_col) for d in range(1, n_row)]
    has_left = chip > 0
    has_right = chip < chips - 1

    far = jnp.maximum(chip, chips - 1 - chip)
    near = chips - 1 - far
    toward = jnp.where(2 * chip < chips - 1, 1, -1)

    def place(i):
        r = i % chips
        later = (r == chips - 1) & (i < steps - 1)
        earlier = (r == 0) & (i > 0)
        i = i + jnp.where(later, 1, 0) - jnp.where(earlier, 1, 0)
        part = i // chips
        s = i - part * chips
        s2 = s - (far - near)
        paired = chip + (near - s2 // 2) * (1 - 2 * (s2 % 2))
        dest = jnp.where(s < far - near, chip + toward * (far - s), paired)
        return part, dest

    eye = lax.broadcasted_iota(jnp.int32, (blk, blk), 0) == lax.broadcasted_iota(
        jnp.int32, (blk, blk), 1
    )

    def to_row(square):
        return jnp.sum(jnp.where(eye, square, 0.0), axis=0, keepdims=True)

    def to_col(row):
        return jnp.sum(jnp.where(eye, jnp.broadcast_to(row, (blk, blk)), 0.0), axis=1, keepdims=True)

    def fetch(group, slot):
        copies = []
        for u in range(GROUP):
            part, dest = place(group * GROUP + u)
            for which in range(2):
                pick = core if which == 0 else 1 - core
                start = pl.multiple_of((dest * 2 + pick) * nodes + part * sub, sub)
                copies.append(
                    pltpu.make_async_copy(
                        a_ref.at[pl.ds(start, sub), :],
                        abuf.at[slot, pl.ds((which * GROUP + u) * sub, sub), :],
                        a_sem.at[slot, which * GROUP + u],
                    )
                )
        return copies

    def remote(src, dst, send, recv, device):
        return pltpu.make_async_remote_copy(
            src_ref=src,
            dst_ref=dst,
            send_sem=send,
            recv_sem=recv,
            device_id=device,
            device_id_type=MESH,
        )

    for copy in fetch(0, 0):
        copy.start()

    barrier = pltpu.get_barrier_semaphore()
    for device in [sibling] + peers:
        pl.semaphore_signal(barrier, inc=1, device_id=device, device_id_type=MESH)

    @pl.when(has_left)
    def _():
        pl.semaphore_signal(barrier, inc=1, device_id=left, device_id_type=MESH)

    @pl.when(has_right)
    def _():
        pl.semaphore_signal(barrier, inc=1, device_id=right, device_id_type=MESH)

    panel1[:, f_in:] = jnp.ones((n_row * nodes, panel1.shape[1] - f_in), BF16)
    panel1[pl.ds(pl.multiple_of(my_row * nodes, nodes), nodes), :f_in] = x_ref[...]

    pl.semaphore_wait(barrier, n_row + jnp.minimum(chip, 1) + jnp.minimum(chips - 1 - chip, 1))

    def part1(row, part):
        rows = pl.ds(pl.multiple_of(row * nodes + part * sub, sub), sub)
        return panel1.at[rows, pl.ds(0, f_in)]

    def part2(row, part):
        return panel2.at[pl.ds(pl.multiple_of(row * nodes + part * sub, sub), sub), :]

    def part3(row, part):
        return panel3.at[pl.ds(row * dev_blocks + part * sub_blocks, sub_blocks)]

    def share(stage, view, part):
        for d in range(1, n_row):
            remote(
                view(my_row, part),
                view(my_row, part),
                g_send.at[stage, d - 1, part],
                g_recv.at[stage, d - 1, part],
                peers[d - 1],
            ).start()

    def arrived_from(stage, view, d):
        source = lax.rem(my_row + n_row - d, n_row)
        for part in range(SUBS):
            where = view(source, part)
            remote(
                where, where, g_send.at[stage, d - 1, part], g_recv.at[stage, d - 1, part], sibling
            ).wait_recv()

    def shared(stage, view):
        for d in range(1, n_row):
            for part in range(SUBS):
                where = view(my_row, part)
                remote(
                    where, where, g_send.at[stage, d - 1, part], g_recv.at[stage, d - 1, part], sibling
                ).wait_send()

    for part in range(SUBS):
        share(0, part1, part)

    def aggregate(layer, panel, view, own, tot, sib_out, sib_in, hop_out, left_in, right_in, finish):
        def store(dst, value):
            if layer == 1:
                dst[...] = value[...].astype(dst.dtype)
                return
            dst[:sub, :] = value[:, :f_in].astype(dst.dtype)
            lane = lax.broadcasted_iota(jnp.int32, (DEG_ROWS, blk), 0)
            degree = jnp.zeros((DEG_ROWS, blk), F32)
            for b in range(sub_blocks):
                row = to_row(value[b * blk : (b + 1) * blk, f_in : f_in + blk])
                degree = jnp.where(lane == b, jnp.broadcast_to(row, (DEG_ROWS, blk)), degree)
            dst[sub:, :] = degree.astype(dst.dtype)

        def sib_copy(at):
            return remote(
                sib_out.at[at], sib_in.at[at], sib_send.at[layer, at], sib_recv.at[layer, at], sibling
            )

        def right_copy(at, device):
            return remote(
                hop_out.at[at], left_in.at[at], hop_send.at[layer, at], left_recv.at[layer, at], device
            )

        def left_copy(at, device):
            return remote(
                hop_out.at[at], right_in.at[at], hop_send.at[layer, at], right_recv.at[layer, at], device
            )

        groups = steps // GROUP

        def multiply(group, slot):
            prod[...] = jnp.zeros_like(prod)

            def add_panel(d, carry):
                @pl.when((group == 0) & (d > 0))
                def _():
                    arrived_from(layer, view, d)

                source = lax.rem(my_row + n_row - d, n_row)
                span = pl.ds(pl.multiple_of(source * nodes, nodes), nodes)
                prod[...] += jnp.dot(
                    abuf[slot, :, span], panel[span, :], preferred_element_type=F32
                )
                return carry

            lax.fori_loop(0, n_row, add_panel, 0)

        def body(group, carry):
            @pl.when(group < groups)
            def _():
                slot = group % 2

                @pl.when(group + 1 < groups)
                def _():
                    for copy in fetch(group + 1, (group + 1) % 2):
                        copy.start()

                for copy in fetch(group, slot):
                    copy.wait()
                multiply(group, slot)
                for u in range(GROUP):
                    part, dest = place(group * GROUP + u)
                    at = part * chips + dest
                    first = (GROUP + u) * sub
                    store(sib_out.at[at], prod.at[first : first + sub])
                    sib_copy(at).start()
                for u in range(GROUP):
                    store(own.at[slot * GROUP + u], prod.at[u * sub : (u + 1) * sub])

            def reduce(u, carry):
                j = (group - 1) * GROUP + u
                part, dest = place(j)
                at = part * chips + dest
                sib_copy(at).wait_recv()
                mine = own.at[((group - 1) % 2) * GROUP + u]

                def forward(copy, arrived, has_up, device):
                    @pl.when(has_up)
                    def _():
                        copy(at, sibling).wait_recv()
                        hop_out[at] = (
                            mine[...] + sib_in[at].astype(F32) + arrived[at].astype(F32)
                        ).astype(BF16)

                    @pl.when(jnp.logical_not(has_up))
                    def _():
                        hop_out[at] = (mine[...] + sib_in[at].astype(F32)).astype(BF16)

                    copy(at, device).start()

                @pl.when(dest > chip)
                def _():
                    forward(right_copy, left_in, has_left, right)

                @pl.when(dest < chip)
                def _():
                    forward(left_copy, right_in, has_right, left)

                @pl.when(dest == chip)
                def _():
                    tot[...] = mine[...] + sib_in[at].astype(F32)

                    @pl.when(has_left)
                    def _():
                        right_copy(at, sibling).wait_recv()
                        tot[...] += left_in[at].astype(F32)

                    @pl.when(has_right)
                    def _():
                        left_copy(at, sibling).wait_recv()
                        tot[...] += right_in[at].astype(F32)

                    finish(part)

                return carry

            @pl.when(group >= 1)
            def _():
                lax.fori_loop(0, GROUP, reduce, 0)

            return carry

        lax.fori_loop(0, groups + 1, body, 0)

        def drain():
            def one(i, carry):
                part, dest = place(i)
                at = part * chips + dest
                sib_copy(at).wait_send()

                @pl.when(dest != chip)
                def _():
                    right_copy(at, sibling).wait_send()

                return carry

            lax.fori_loop(0, steps, one, 0)

        return drain

    def finish1(part):
        for b in range(sub_blocks):
            rows = pl.ds(pl.multiple_of(part * sub + b * blk, blk), blk)
            scale = lax.rsqrt(1.0 + to_col(tot1[sub + b : sub + b + 1, :]))
            scale_ref[rows, :] = jnp.broadcast_to(scale, (blk, blk))
            mean = tot1[b * blk : (b + 1) * blk, :] * scale
            high = mean.astype(BF16)
            low = (mean - high.astype(F32)).astype(BF16)
            before = jnp.dot(high, w1_ref[:, :hid], preferred_element_type=F32)
            before += jnp.dot(low, w1_ref[:, :hid], preferred_element_type=F32)
            before += jnp.dot(x_ref[rows, :], w1_ref[:, hid:], preferred_element_type=F32)
            hidden = jnp.tanh(before).astype(BF16)
            h1_ref[rows, :] = hidden
            mine = pl.ds(pl.multiple_of(my_row * nodes + part * sub + b * blk, blk), blk)
            panel2[mine, :] = jnp.dot(
                hidden, w2_ref[:, :hid], preferred_element_type=F32
            ).astype(BF16)
        share(1, part2, part)

    drain1 = aggregate(
        0, panel1, part1, own1, tot1, sib_out1, sib_in1, hop_out1, left_in1, right_in1, finish1
    )
    for copy in fetch(0, 0):
        copy.start()

    def finish2(part):
        for b in range(sub_blocks):
            rows = pl.ds(pl.multiple_of(part * sub + b * blk, blk), blk)
            before = jnp.dot(h1_ref[rows, :], w2_ref[:, hid:], preferred_element_type=F32)
            before += tot2[b * blk : (b + 1) * blk, :] * scale_ref[rows, 0:1] + b2_ref[...]
            panel3[my_row * dev_blocks + part * sub_blocks + b] = jnp.tanh(before).astype(BF16)
        share(2, part3, part)

    drain2 = aggregate(
        1, panel2, part2, own2, tot2, sib_out2, sib_in2, hop_out2, left_in2, right_in2, finish2
    )

    def attr_block(b, carry):
        rows = pl.ds(pl.multiple_of(b * blk, blk), blk)
        rebuilt = jnp.dot(
            panel3[my_row * dev_blocks + b], wa_ref[...], preferred_element_type=F32
        )
        diff = rebuilt + ba_ref[...] - x_ref[rows, :].astype(F32)
        error = jnp.sqrt(jnp.mean(diff * diff, axis=1, keepdims=True) + epsilon)
        attr_ref[rows, :] = jnp.broadcast_to(error, (blk, blk))
        return carry

    lax.fori_loop(0, dev_blocks, attr_block, 0)
    drain1()
    drain2()
    for stage, view in enumerate((part1, part2, part3)):
        shared(stage, view)
    for d in range(1, n_row):
        arrived_from(2, part3, d)

    pair_count = pair_ref.shape[1]

    def decode(b, carry):
        rows = pl.ds(pl.multiple_of(b * blk, blk), blk)
        mine = panel3[my_row * dev_blocks + b]
        total = jnp.zeros((blk, blk), F32)
        for j in range(pair_count):
            logits = lax.dot_general(
                mine,
                panel3[pair_ref[b, j]],
                (((1,), (1,)), ((), ())),
                preferred_element_type=F32,
            ) * hid ** (-0.5)
            diff = jax.nn.sigmoid(logits) - target_ref[rows, j, :].astype(F32)
            total += diff * diff
        mean = jnp.sum(total, axis=1, keepdims=True) * (1.0 / (pair_count * blk))
        score = mix_alpha * attr_ref[rows, :] + (1.0 - mix_alpha) * jnp.sqrt(mean + epsilon)
        out_ref[pl.ds(b, 1), :] = to_row(score)
        return carry

    lax.fori_loop(0, dev_blocks, decode, 0)


def per_device(
    attributes,
    adj_values,
    adj_rows,
    adj_cols,
    adj_count,
    pair_ids,
    struct_target,
    w_first,
    w_rest,
    layer_bias,
    w_attr,
    attr_bias,
):
    n_row = lax.axis_size("row")
    n_col = lax.axis_size("col")
    nodes, f_in = attributes.shape
    blk = adj_values.shape[3]
    hid = w_rest.shape[1]
    row_blocks = n_col * nodes // blk
    col_blocks = n_row * nodes // blk
    dense = dense_tile(
        adj_values[0, 0], adj_rows, adj_cols, adj_count, row_blocks, col_blocks
    )
    sub = nodes // SUBS
    steps = SUBS * (n_col // 2)
    wide = 2 * blk
    vmem = pl.BlockSpec(memory_space=pltpu.VMEM)
    ring1 = pltpu.VMEM((steps, sub + DEG_ROWS, f_in), BF16)
    ring2 = pltpu.VMEM((steps, sub, hid), BF16)
    scores = pl.pallas_call(
        functools.partial(graph_kernel, n_row, n_col),
        out_shape=jax.ShapeDtypeStruct((nodes // blk, blk), F32),
        in_specs=[
            vmem,
            pl.BlockSpec(memory_space=pl.ANY),
            pl.BlockSpec(memory_space=pltpu.SMEM),
        ]
        + [vmem] * 6,
        out_specs=vmem,
        scratch_shapes=[
            pltpu.VMEM((n_row * nodes, f_in + blk), BF16),
            pltpu.VMEM((n_row * nodes, hid), BF16),
            pltpu.VMEM((col_blocks, blk, hid), BF16),
            pltpu.VMEM((2, 2 * GROUP * sub, col_blocks * blk), BF16),
            pltpu.VMEM((2 * GROUP, sub + DEG_ROWS, f_in), F32),
            pltpu.VMEM((2 * GROUP, sub, hid), F32),
            pltpu.VMEM((sub + DEG_ROWS, f_in), F32),
            pltpu.VMEM((sub, hid), F32),
            pltpu.VMEM((nodes, hid), BF16),
            pltpu.VMEM((nodes, blk), F32),
            pltpu.VMEM((nodes, blk), F32),
        ]
        + [ring1] * 5
        + [ring2] * 5
        + [
            pltpu.SemaphoreType.DMA((2, 2 * GROUP)),
            pltpu.SemaphoreType.DMA((3, n_row - 1, SUBS)),
            pltpu.SemaphoreType.DMA((3, n_row - 1, SUBS)),
            pltpu.SemaphoreType.DMA((2, steps)),
            pltpu.SemaphoreType.DMA((2, steps)),
            pltpu.SemaphoreType.DMA((2, steps)),
            pltpu.SemaphoreType.DMA((2, steps)),
            pltpu.SemaphoreType.DMA((2, steps)),
            pltpu.VMEM((2 * GROUP * sub, wide), F32),
        ],
        compiler_params=pltpu.CompilerParams(
            collective_id=0, has_side_effects=True, vmem_limit_bytes=56 * 1024 * 1024
        ),
        name="graph_layers",
    )(
        attributes,
        dense,
        pair_ids,
        struct_target,
        w_first,
        w_rest[0],
        layer_bias,
        w_attr,
        attr_bias.reshape(1, -1),
    )
    return scores.reshape(nodes)


def solution(mesh):
    return jax.shard_map(
        per_device,
        mesh=mesh,
        in_specs=(
            P(("row", "col"), None),
            P("row", "col", None, None, None),
            P("row", "col", None),
            P("row", "col", None),
            P("row", "col"),
            P(("row", "col"), None),
            P(("row", "col"), None, None),
            P(),
            P(),
            P(),
            P(),
            P(),
        ),
        out_specs=P(("row", "col")),
        check_vma=False,
    )
```

```python
import functools

import jax
import jax.numpy as jnp
from jax import lax
from jax.experimental import pallas as pl
from jax.experimental.pallas import tpu as pltpu
from jax.sharding import PartitionSpec as P

epsilon = 1e-06
mix_alpha = 0.8
MESH = pl.DeviceIdType.MESH
F32 = jnp.float32
BF16 = jnp.bfloat16
SUBS = 2
GROUP = 1
OWN_LAG = 2
DEG_ROWS = 16


def dense_kernel(part_blocks, rows_ref, cols_ref, count_ref, vals_hbm, out_ref, vals_ref, lists, sizes, sem):
    part = pl.program_id(0)
    blk = vals_ref.shape[1]
    load = pltpu.make_async_copy(vals_hbm, vals_ref, sem)

    @pl.when(part == 0)
    def _():
        load.start()
        for q in range(sizes.shape[0]):
            sizes[q] = 0

        def assign(k, carry):
            q = lax.div(rows_ref[0, 0, k], part_blocks)
            n = sizes[q]
            lists[q, n] = k
            sizes[q] = n + 1
            return carry

        lax.fori_loop(0, count_ref[0, 0], assign, 0)

    out_ref[...] = jnp.zeros_like(out_ref)

    @pl.when(part == 0)
    def _():
        load.wait()

    def add_slot(n, carry):
        k = lists[part, n]
        row = rows_ref[0, 0, k] - part * part_blocks
        where_r = pl.ds(pl.multiple_of(row * blk, blk), blk)
        where_c = pl.ds(pl.multiple_of(cols_ref[0, 0, k] * blk, blk), blk)
        out_ref[where_r, where_c] = out_ref[where_r, where_c] + vals_ref[k]
        return carry

    lax.fori_loop(0, sizes[part], add_slot, 0)


def dense_tile(vals, row_ids, col_ids, count, row_blocks, col_blocks):
    cap, blk, _ = vals.shape
    part_blocks = 4
    parts = row_blocks // part_blocks
    dense_bytes = row_blocks * col_blocks * blk * blk * 2
    return pl.pallas_call(
        functools.partial(dense_kernel, part_blocks),
        grid=(parts,),
        in_specs=[pl.BlockSpec(memory_space=pltpu.SMEM)] * 3
        + [pl.BlockSpec(memory_space=pl.ANY)],
        out_specs=pl.BlockSpec((part_blocks * blk, col_blocks * blk), lambda i: (i, 0)),
        scratch_shapes=[
            pltpu.VMEM((cap, blk, blk), vals.dtype),
            pltpu.SMEM((parts, cap), jnp.int32),
            pltpu.SMEM((parts,), jnp.int32),
            pltpu.SemaphoreType.DMA,
        ],
        out_shape=jax.ShapeDtypeStruct((row_blocks * blk, col_blocks * blk), vals.dtype),
        compiler_params=pltpu.CompilerParams(vmem_limit_bytes=48 * 1024 * 1024),
        cost_estimate=pl.CostEstimate(
            flops=dense_bytes, bytes_accessed=2 * dense_bytes, transcendentals=0
        ),
        name="dense_tile",
    )(row_ids, col_ids, count, vals)


def graph_kernel(
    n_row,
    n_col,
    x_ref,
    a_ref,
    pair_ref,
    target_ref,
    w1_ref,
    w2_ref,
    b2_ref,
    wa_ref,
    ba_ref,
    out_ref,
    panel1,
    panel2,
    panel3,
    abuf,
    own1,
    own2,
    tot1,
    tot2,
    h1_ref,
    scale_ref,
    attr_ref,
    sib_out1,
    sib_in1,
    hop_out1,
    left_in1,
    right_in1,
    sib_out2,
    sib_in2,
    hop_out2,
    left_in2,
    right_in2,
    a_sem,
    g_send,
    g_recv,
    sib_send,
    sib_recv,
    hop_send,
    left_recv,
    right_recv,
    prod,
):
    my_row = lax.axis_index("row")
    my_col = lax.axis_index("col")
    chips = n_col // 2
    chip = my_col // 2
    core = my_col % 2
    nodes, f_in = x_ref.shape
    hid = w2_ref.shape[0]
    blk = panel3.shape[1]
    sub = nodes // SUBS
    sub_blocks = sub // blk
    dev_blocks = nodes // blk
    steps = SUBS * chips

    sibling = (my_row, chip * 2 + 1 - core)
    right = (my_row, my_col + 2)
    left = (my_row, my_col - 2)
    peers = [(lax.rem(my_row + d, n_row), my_col) for d in range(1, n_row)]
    has_left = chip > 0
    has_right = chip < chips - 1

    far = jnp.maximum(chip, chips - 1 - chip)
    near = chips - 1 - far
    toward = jnp.where(2 * chip < chips - 1, 1, -1)

    def place(i):
        lag = min(OWN_LAG, chips - 1)
        first = i < chips - 1
        j = jnp.maximum(i - (chips - 1), 0)
        turn = j // chips
        r = j % chips
        is_own = jnp.logical_not(first) & ((r == lag) | (i == steps - 1))
        part = jnp.where(first, 0, jnp.where(is_own, turn, turn + 1))
        later = jnp.where(is_own, chips - 1, jnp.where(r < lag, r, r - 1))
        s = jnp.where(first, i, later)
        s2 = s - (far - near)
        paired = chip + (near - s2 // 2) * (1 - 2 * (s2 % 2))
        dest = jnp.where(s < far - near, chip + toward * (far - s), paired)
        return part, dest

    eye = lax.broadcasted_iota(jnp.int32, (blk, blk), 0) == lax.broadcasted_iota(
        jnp.int32, (blk, blk), 1
    )

    def to_row(square):
        return jnp.sum(jnp.where(eye, square, 0.0), axis=0, keepdims=True)

    def to_col(row):
        return jnp.sum(jnp.where(eye, jnp.broadcast_to(row, (blk, blk)), 0.0), axis=1, keepdims=True)

    def fetch(group, slot):
        copies = []
        for u in range(GROUP):
            part, dest = place(group * GROUP + u)
            for which in range(2):
                pick = core if which == 0 else 1 - core
                start = pl.multiple_of((dest * 2 + pick) * nodes + part * sub, sub)
                copies.append(
                    pltpu.make_async_copy(
                        a_ref.at[pl.ds(start, sub), :],
                        abuf.at[slot, pl.ds((which * GROUP + u) * sub, sub), :],
                        a_sem.at[slot, which * GROUP + u],
                    )
                )
        return copies

    def remote(src, dst, send, recv, device):
        return pltpu.make_async_remote_copy(
            src_ref=src,
            dst_ref=dst,
            send_sem=send,
            recv_sem=recv,
            device_id=device,
            device_id_type=MESH,
        )

    for copy in fetch(0, 0):
        copy.start()

    barrier = pltpu.get_barrier_semaphore()
    for device in [sibling] + peers:
        pl.semaphore_signal(barrier, inc=1, device_id=device, device_id_type=MESH)

    @pl.when(has_left)
    def _():
        pl.semaphore_signal(barrier, inc=1, device_id=left, device_id_type=MESH)

    @pl.when(has_right)
    def _():
        pl.semaphore_signal(barrier, inc=1, device_id=right, device_id_type=MESH)

    panel1[:, f_in:] = jnp.ones((n_row * nodes, panel1.shape[1] - f_in), BF16)
    panel1[pl.ds(pl.multiple_of(my_row * nodes, nodes), nodes), :f_in] = x_ref[...]

    pl.semaphore_wait(barrier, n_row + jnp.minimum(chip, 1) + jnp.minimum(chips - 1 - chip, 1))

    def part1(row, part):
        rows = pl.ds(pl.multiple_of(row * nodes + part * sub, sub), sub)
        return panel1.at[rows, pl.ds(0, f_in)]

    def part2(row, part):
        return panel2.at[pl.ds(pl.multiple_of(row * nodes + part * sub, sub), sub), :]

    def part3(row, part):
        return panel3.at[pl.ds(row * dev_blocks + part * sub_blocks, sub_blocks)]

    def share(stage, view, part):
        for d in range(1, n_row):
            remote(
                view(my_row, part),
                view(my_row, part),
                g_send.at[stage, d - 1, part],
                g_recv.at[stage, d - 1, part],
                peers[d - 1],
            ).start()

    def arrived_from(stage, view, d):
        source = lax.rem(my_row + n_row - d, n_row)
        for part in range(SUBS):
            where = view(source, part)
            remote(
                where, where, g_send.at[stage, d - 1, part], g_recv.at[stage, d - 1, part], sibling
            ).wait_recv()

    def shared(stage, view):
        for d in range(1, n_row):
            for part in range(SUBS):
                where = view(my_row, part)
                remote(
                    where, where, g_send.at[stage, d - 1, part], g_recv.at[stage, d - 1, part], sibling
                ).wait_send()

    for part in range(SUBS):
        share(0, part1, part)

    def aggregate(layer, panel, view, own, tot, sib_out, sib_in, hop_out, left_in, right_in, finish):
        def store(dst, value):
            if layer == 1:
                dst[...] = value[...].astype(dst.dtype)
                return
            dst[:sub, :] = value[:, :f_in].astype(dst.dtype)
            lane = lax.broadcasted_iota(jnp.int32, (DEG_ROWS, blk), 0)
            degree = jnp.zeros((DEG_ROWS, blk), F32)
            for b in range(sub_blocks):
                row = to_row(value[b * blk : (b + 1) * blk, f_in : f_in + blk])
                degree = jnp.where(lane == b, jnp.broadcast_to(row, (DEG_ROWS, blk)), degree)
            dst[sub:, :] = degree.astype(dst.dtype)

        def sib_copy(at):
            return remote(
                sib_out.at[at], sib_in.at[at], sib_send.at[layer, at], sib_recv.at[layer, at], sibling
            )

        def right_copy(at, device):
            return remote(
                hop_out.at[at], left_in.at[at], hop_send.at[layer, at], left_recv.at[layer, at], device
            )

        def left_copy(at, device):
            return remote(
                hop_out.at[at], right_in.at[at], hop_send.at[layer, at], right_recv.at[layer, at], device
            )

        groups = steps // GROUP

        def multiply(group, slot):
            prod[...] = jnp.zeros_like(prod)

            def add_panel(d, carry):
                @pl.when((group == 0) & (d > 0))
                def _():
                    arrived_from(layer, view, d)

                source = lax.rem(my_row + n_row - d, n_row)
                span = pl.ds(pl.multiple_of(source * nodes, nodes), nodes)
                prod[...] += jnp.dot(
                    abuf[slot, :, span], panel[span, :], preferred_element_type=F32
                )
                return carry

            lax.fori_loop(0, n_row, add_panel, 0)

        def body(group, carry):
            @pl.when(group < groups)
            def _():
                slot = group % 2

                @pl.when(group + 1 < groups)
                def _():
                    for copy in fetch(group + 1, (group + 1) % 2):
                        copy.start()

                for copy in fetch(group, slot):
                    copy.wait()
                multiply(group, slot)
                for u in range(GROUP):
                    part, dest = place(group * GROUP + u)
                    at = part * chips + dest
                    first = (GROUP + u) * sub
                    store(sib_out.at[at], prod.at[first : first + sub])
                    sib_copy(at).start()
                for u in range(GROUP):
                    store(own.at[slot * GROUP + u], prod.at[u * sub : (u + 1) * sub])

            def reduce(u, carry):
                j = (group - 1) * GROUP + u
                part, dest = place(j)
                at = part * chips + dest
                sib_copy(at).wait_recv()
                mine = own.at[((group - 1) % 2) * GROUP + u]

                def forward(copy, arrived, has_up, device):
                    @pl.when(has_up)
                    def _():
                        copy(at, sibling).wait_recv()
                        hop_out[at] = (
                            mine[...] + sib_in[at].astype(F32) + arrived[at].astype(F32)
                        ).astype(BF16)

                    @pl.when(jnp.logical_not(has_up))
                    def _():
                        hop_out[at] = (mine[...] + sib_in[at].astype(F32)).astype(BF16)

                    copy(at, device).start()

                @pl.when(dest > chip)
                def _():
                    forward(right_copy, left_in, has_left, right)

                @pl.when(dest < chip)
                def _():
                    forward(left_copy, right_in, has_right, left)

                @pl.when(dest == chip)
                def _():
                    tot[...] = mine[...] + sib_in[at].astype(F32)

                    @pl.when(has_left)
                    def _():
                        right_copy(at, sibling).wait_recv()
                        tot[...] += left_in[at].astype(F32)

                    @pl.when(has_right)
                    def _():
                        left_copy(at, sibling).wait_recv()
                        tot[...] += right_in[at].astype(F32)

                    finish(part)

                return carry

            @pl.when(group >= 1)
            def _():
                lax.fori_loop(0, GROUP, reduce, 0)

            return carry

        lax.fori_loop(0, groups + 1, body, 0)

        def drain():
            def one(i, carry):
                part, dest = place(i)
                at = part * chips + dest
                sib_copy(at).wait_send()

                @pl.when(dest != chip)
                def _():
                    right_copy(at, sibling).wait_send()

                return carry

            lax.fori_loop(0, steps, one, 0)

        return drain

    def finish1(part):
        for b in range(sub_blocks):
            rows = pl.ds(pl.multiple_of(part * sub + b * blk, blk), blk)
            scale = lax.rsqrt(1.0 + to_col(tot1[sub + b : sub + b + 1, :]))
            scale_ref[rows, :] = jnp.broadcast_to(scale, (blk, blk))
            mean = tot1[b * blk : (b + 1) * blk, :] * scale
            high = mean.astype(BF16)
            low = (mean - high.astype(F32)).astype(BF16)
            before = jnp.dot(high, w1_ref[:, :hid], preferred_element_type=F32)
            before += jnp.dot(low, w1_ref[:, :hid], preferred_element_type=F32)
            before += jnp.dot(x_ref[rows, :], w1_ref[:, hid:], preferred_element_type=F32)
            hidden = jnp.tanh(before).astype(BF16)
            h1_ref[rows, :] = hidden
            mine = pl.ds(pl.multiple_of(my_row * nodes + part * sub + b * blk, blk), blk)
            panel2[mine, :] = jnp.dot(
                hidden, w2_ref[:, :hid], preferred_element_type=F32
            ).astype(BF16)
        share(1, part2, part)

    drain1 = aggregate(
        0, panel1, part1, own1, tot1, sib_out1, sib_in1, hop_out1, left_in1, right_in1, finish1
    )
    for copy in fetch(0, 0):
        copy.start()

    def finish2(part):
        for b in range(sub_blocks):
            rows = pl.ds(pl.multiple_of(part * sub + b * blk, blk), blk)
            before = jnp.dot(h1_ref[rows, :], w2_ref[:, hid:], preferred_element_type=F32)
            before += tot2[b * blk : (b + 1) * blk, :] * scale_ref[rows, 0:1] + b2_ref[...]
            panel3[my_row * dev_blocks + part * sub_blocks + b] = jnp.tanh(before).astype(BF16)
        share(2, part3, part)

    drain2 = aggregate(
        1, panel2, part2, own2, tot2, sib_out2, sib_in2, hop_out2, left_in2, right_in2, finish2
    )

    def attr_block(b, carry):
        rows = pl.ds(pl.multiple_of(b * blk, blk), blk)
        rebuilt = jnp.dot(
            panel3[my_row * dev_blocks + b], wa_ref[...], preferred_element_type=F32
        )
        diff = rebuilt + ba_ref[...] - x_ref[rows, :].astype(F32)
        error = jnp.sqrt(jnp.mean(diff * diff, axis=1, keepdims=True) + epsilon)
        attr_ref[rows, :] = jnp.broadcast_to(error, (blk, blk))
        return carry

    lax.fori_loop(0, dev_blocks, attr_block, 0)
    drain1()
    drain2()
    for stage, view in enumerate((part1, part2, part3)):
        shared(stage, view)
    for d in range(1, n_row):
        arrived_from(2, part3, d)

    pair_count = pair_ref.shape[1]

    def decode(b, carry):
        rows = pl.ds(pl.multiple_of(b * blk, blk), blk)
        mine = panel3[my_row * dev_blocks + b]
        total = jnp.zeros((blk, blk), F32)
        for j in range(pair_count):
            logits = lax.dot_general(
                mine,
                panel3[pair_ref[b, j]],
                (((1,), (1,)), ((), ())),
                preferred_element_type=F32,
            ) * hid ** (-0.5)
            diff = jax.nn.sigmoid(logits) - target_ref[rows, j, :].astype(F32)
            total += diff * diff
        mean = jnp.sum(total, axis=1, keepdims=True) * (1.0 / (pair_count * blk))
        score = mix_alpha * attr_ref[rows, :] + (1.0 - mix_alpha) * jnp.sqrt(mean + epsilon)
        out_ref[pl.ds(b, 1), :] = to_row(score)
        return carry

    lax.fori_loop(0, dev_blocks, decode, 0)


def per_device(
    attributes,
    adj_values,
    adj_rows,
    adj_cols,
    adj_count,
    pair_ids,
    struct_target,
    w_first,
    w_rest,
    layer_bias,
    w_attr,
    attr_bias,
):
    n_row = lax.axis_size("row")
    n_col = lax.axis_size("col")
    nodes, f_in = attributes.shape
    blk = adj_values.shape[3]
    hid = w_rest.shape[1]
    row_blocks = n_col * nodes // blk
    col_blocks = n_row * nodes // blk
    dense = dense_tile(
        adj_values[0, 0], adj_rows, adj_cols, adj_count, row_blocks, col_blocks
    )
    sub = nodes // SUBS
    steps = SUBS * (n_col // 2)
    wide = 2 * blk
    vmem = pl.BlockSpec(memory_space=pltpu.VMEM)
    ring1 = pltpu.VMEM((steps, sub + DEG_ROWS, f_in), BF16)
    ring2 = pltpu.VMEM((steps, sub, hid), BF16)
    scores = pl.pallas_call(
        functools.partial(graph_kernel, n_row, n_col),
        out_shape=jax.ShapeDtypeStruct((nodes // blk, blk), F32),
        in_specs=[
            vmem,
            pl.BlockSpec(memory_space=pl.ANY),
            pl.BlockSpec(memory_space=pltpu.SMEM),
        ]
        + [vmem] * 6,
        out_specs=vmem,
        scratch_shapes=[
            pltpu.VMEM((n_row * nodes, f_in + blk), BF16),
            pltpu.VMEM((n_row * nodes, hid), BF16),
            pltpu.VMEM((col_blocks, blk, hid), BF16),
            pltpu.VMEM((2, 2 * GROUP * sub, col_blocks * blk), BF16),
            pltpu.VMEM((2 * GROUP, sub + DEG_ROWS, f_in), F32),
            pltpu.VMEM((2 * GROUP, sub, hid), F32),
            pltpu.VMEM((sub + DEG_ROWS, f_in), F32),
            pltpu.VMEM((sub, hid), F32),
            pltpu.VMEM((nodes, hid), BF16),
            pltpu.VMEM((nodes, blk), F32),
            pltpu.VMEM((nodes, blk), F32),
        ]
        + [ring1] * 5
        + [ring2] * 5
        + [
            pltpu.SemaphoreType.DMA((2, 2 * GROUP)),
            pltpu.SemaphoreType.DMA((3, n_row - 1, SUBS)),
            pltpu.SemaphoreType.DMA((3, n_row - 1, SUBS)),
            pltpu.SemaphoreType.DMA((2, steps)),
            pltpu.SemaphoreType.DMA((2, steps)),
            pltpu.SemaphoreType.DMA((2, steps)),
            pltpu.SemaphoreType.DMA((2, steps)),
            pltpu.SemaphoreType.DMA((2, steps)),
            pltpu.VMEM((2 * GROUP * sub, wide), F32),
        ],
        compiler_params=pltpu.CompilerParams(
            collective_id=0, has_side_effects=True, vmem_limit_bytes=56 * 1024 * 1024
        ),
        name="graph_layers",
    )(
        attributes,
        dense,
        pair_ids,
        struct_target,
        w_first,
        w_rest[0],
        layer_bias,
        w_attr,
        attr_bias.reshape(1, -1),
    )
    return scores.reshape(nodes)


def solution(mesh):
    return jax.shard_map(
        per_device,
        mesh=mesh,
        in_specs=(
            P(("row", "col"), None),
            P("row", "col", None, None, None),
            P("row", "col", None),
            P("row", "col", None),
            P("row", "col"),
            P(("row", "col"), None),
            P(("row", "col"), None, None),
            P(),
            P(),
            P(),
            P(),
            P(),
        ),
        out_specs=P(("row", "col")),
        check_vma=False,
    )
```

```python
import functools

import jax
import jax.numpy as jnp
from jax import lax
from jax.experimental import pallas as pl
from jax.experimental.pallas import tpu as pltpu
from jax.sharding import PartitionSpec as P

epsilon = 1e-06
mix_alpha = 0.8
MESH = pl.DeviceIdType.MESH
F32 = jnp.float32
BF16 = jnp.bfloat16
SUBS = 2
GROUP = 1
OWN_LAG = 2
SLOTS = 4
DEG_ROWS = 16


def dense_kernel(part_blocks, rows_ref, cols_ref, count_ref, vals_hbm, out_ref, vals_ref, lists, sizes, sem):
    part = pl.program_id(0)
    blk = vals_ref.shape[1]
    load = pltpu.make_async_copy(vals_hbm, vals_ref, sem)

    @pl.when(part == 0)
    def _():
        load.start()
        for q in range(sizes.shape[0]):
            sizes[q] = 0

        def assign(k, carry):
            q = lax.div(rows_ref[0, 0, k], part_blocks)
            n = sizes[q]
            lists[q, n] = k
            sizes[q] = n + 1
            return carry

        lax.fori_loop(0, count_ref[0, 0], assign, 0)

    out_ref[...] = jnp.zeros_like(out_ref)

    @pl.when(part == 0)
    def _():
        load.wait()

    def add_slot(n, carry):
        k = lists[part, n]
        row = rows_ref[0, 0, k] - part * part_blocks
        where_r = pl.ds(pl.multiple_of(row * blk, blk), blk)
        where_c = pl.ds(pl.multiple_of(cols_ref[0, 0, k] * blk, blk), blk)
        out_ref[where_r, where_c] = out_ref[where_r, where_c] + vals_ref[k]
        return carry

    lax.fori_loop(0, sizes[part], add_slot, 0)


def dense_tile(vals, row_ids, col_ids, count, row_blocks, col_blocks):
    cap, blk, _ = vals.shape
    part_blocks = 4
    parts = row_blocks // part_blocks
    dense_bytes = row_blocks * col_blocks * blk * blk * 2
    return pl.pallas_call(
        functools.partial(dense_kernel, part_blocks),
        grid=(parts,),
        in_specs=[pl.BlockSpec(memory_space=pltpu.SMEM)] * 3
        + [pl.BlockSpec(memory_space=pl.ANY)],
        out_specs=pl.BlockSpec((part_blocks * blk, col_blocks * blk), lambda i: (i, 0)),
        scratch_shapes=[
            pltpu.VMEM((cap, blk, blk), vals.dtype),
            pltpu.SMEM((parts, cap), jnp.int32),
            pltpu.SMEM((parts,), jnp.int32),
            pltpu.SemaphoreType.DMA,
        ],
        out_shape=jax.ShapeDtypeStruct((row_blocks * blk, col_blocks * blk), vals.dtype),
        compiler_params=pltpu.CompilerParams(vmem_limit_bytes=48 * 1024 * 1024),
        cost_estimate=pl.CostEstimate(
            flops=dense_bytes, bytes_accessed=2 * dense_bytes, transcendentals=0
        ),
        name="dense_tile",
    )(row_ids, col_ids, count, vals)


def graph_kernel(
    n_row,
    n_col,
    x_ref,
    a_ref,
    pair_ref,
    target_ref,
    w1_ref,
    w2_ref,
    b2_ref,
    wa_ref,
    ba_ref,
    out_ref,
    panel1,
    panel2,
    panel3,
    abuf,
    own1,
    own2,
    tot1,
    tot2,
    h1_ref,
    scale_ref,
    attr_ref,
    sib_out1,
    sib_in1,
    hop_out1,
    left_in1,
    right_in1,
    sib_out2,
    sib_in2,
    hop_out2,
    left_in2,
    right_in2,
    a_sem,
    g_send,
    g_recv,
    sib_send,
    sib_recv,
    hop_send,
    left_recv,
    right_recv,
    prod,
):
    my_row = lax.axis_index("row")
    my_col = lax.axis_index("col")
    chips = n_col // 2
    chip = my_col // 2
    core = my_col % 2
    nodes, f_in = x_ref.shape
    hid = w2_ref.shape[0]
    blk = panel3.shape[1]
    sub = nodes // SUBS
    sub_blocks = sub // blk
    dev_blocks = nodes // blk
    steps = SUBS * chips

    sibling = (my_row, chip * 2 + 1 - core)
    right = (my_row, my_col + 2)
    left = (my_row, my_col - 2)
    peers = [(lax.rem(my_row + d, n_row), my_col) for d in range(1, n_row)]
    has_left = chip > 0
    has_right = chip < chips - 1

    far = jnp.maximum(chip, chips - 1 - chip)
    near = chips - 1 - far
    toward = jnp.where(2 * chip < chips - 1, 1, -1)

    def place(i):
        lag = min(OWN_LAG, chips - 1)
        first = i < chips - 1
        j = jnp.maximum(i - (chips - 1), 0)
        turn = j // chips
        r = j % chips
        is_own = jnp.logical_not(first) & ((r == lag) | (i == steps - 1))
        part = jnp.where(first, 0, jnp.where(is_own, turn, turn + 1))
        later = jnp.where(is_own, chips - 1, jnp.where(r < lag, r, r - 1))
        s = jnp.where(first, i, later)
        s2 = s - (far - near)
        paired = chip + (near - s2 // 2) * (1 - 2 * (s2 % 2))
        dest = jnp.where(s < far - near, chip + toward * (far - s), paired)
        return part, dest

    eye = lax.broadcasted_iota(jnp.int32, (blk, blk), 0) == lax.broadcasted_iota(
        jnp.int32, (blk, blk), 1
    )

    def to_row(square):
        return jnp.sum(jnp.where(eye, square, 0.0), axis=0, keepdims=True)

    def to_col(row):
        return jnp.sum(jnp.where(eye, jnp.broadcast_to(row, (blk, blk)), 0.0), axis=1, keepdims=True)

    def fetch(group, slot):
        copies = []
        for u in range(GROUP):
            part, dest = place(group * GROUP + u)
            for which in range(2):
                pick = core if which == 0 else 1 - core
                start = pl.multiple_of((dest * 2 + pick) * nodes + part * sub, sub)
                copies.append(
                    pltpu.make_async_copy(
                        a_ref.at[pl.ds(start, sub), :],
                        abuf.at[slot, pl.ds((which * GROUP + u) * sub, sub), :],
                        a_sem.at[slot, which * GROUP + u],
                    )
                )
        return copies

    def remote(src, dst, send, recv, device):
        return pltpu.make_async_remote_copy(
            src_ref=src,
            dst_ref=dst,
            send_sem=send,
            recv_sem=recv,
            device_id=device,
            device_id_type=MESH,
        )

    for early in range(min(SLOTS - 1, steps // GROUP)):
        for copy in fetch(early, early):
            copy.start()

    barrier = pltpu.get_barrier_semaphore()
    for device in [sibling] + peers:
        pl.semaphore_signal(barrier, inc=1, device_id=device, device_id_type=MESH)

    @pl.when(has_left)
    def _():
        pl.semaphore_signal(barrier, inc=1, device_id=left, device_id_type=MESH)

    @pl.when(has_right)
    def _():
        pl.semaphore_signal(barrier, inc=1, device_id=right, device_id_type=MESH)

    panel1[:, f_in:] = jnp.ones((n_row * nodes, panel1.shape[1] - f_in), BF16)
    panel1[pl.ds(pl.multiple_of(my_row * nodes, nodes), nodes), :f_in] = x_ref[...]

    pl.semaphore_wait(barrier, n_row + jnp.minimum(chip, 1) + jnp.minimum(chips - 1 - chip, 1))

    def part1(row, part):
        rows = pl.ds(pl.multiple_of(row * nodes + part * sub, sub), sub)
        return panel1.at[rows, pl.ds(0, f_in)]

    def part2(row, part):
        return panel2.at[pl.ds(pl.multiple_of(row * nodes + part * sub, sub), sub), :]

    def part3(row, part):
        return panel3.at[pl.ds(row * dev_blocks + part * sub_blocks, sub_blocks)]

    def share(stage, view, part):
        for d in range(1, n_row):
            remote(
                view(my_row, part),
                view(my_row, part),
                g_send.at[stage, d - 1, part],
                g_recv.at[stage, d - 1, part],
                peers[d - 1],
            ).start()

    def arrived_from(stage, view, d):
        source = lax.rem(my_row + n_row - d, n_row)
        for part in range(SUBS):
            where = view(source, part)
            remote(
                where, where, g_send.at[stage, d - 1, part], g_recv.at[stage, d - 1, part], sibling
            ).wait_recv()

    def shared(stage, view):
        for d in range(1, n_row):
            for part in range(SUBS):
                where = view(my_row, part)
                remote(
                    where, where, g_send.at[stage, d - 1, part], g_recv.at[stage, d - 1, part], sibling
                ).wait_send()

    for part in range(SUBS):
        share(0, part1, part)

    def aggregate(layer, panel, view, own, tot, sib_out, sib_in, hop_out, left_in, right_in, finish):
        def store(dst, value):
            if layer == 1:
                dst[...] = value[...].astype(dst.dtype)
                return
            dst[:sub, :] = value[:, :f_in].astype(dst.dtype)
            lane = lax.broadcasted_iota(jnp.int32, (DEG_ROWS, blk), 0)
            degree = jnp.zeros((DEG_ROWS, blk), F32)
            for b in range(sub_blocks):
                row = to_row(value[b * blk : (b + 1) * blk, f_in : f_in + blk])
                degree = jnp.where(lane == b, jnp.broadcast_to(row, (DEG_ROWS, blk)), degree)
            dst[sub:, :] = degree.astype(dst.dtype)

        def sib_copy(at):
            return remote(
                sib_out.at[at], sib_in.at[at], sib_send.at[layer, at], sib_recv.at[layer, at], sibling
            )

        def right_copy(at, device):
            return remote(
                hop_out.at[at], left_in.at[at], hop_send.at[layer, at], left_recv.at[layer, at], device
            )

        def left_copy(at, device):
            return remote(
                hop_out.at[at], right_in.at[at], hop_send.at[layer, at], right_recv.at[layer, at], device
            )

        groups = steps // GROUP

        def multiply(group, slot):
            prod[...] = jnp.zeros_like(prod)

            def add_panel(d, carry):
                @pl.when((group == 0) & (d > 0))
                def _():
                    arrived_from(layer, view, d)

                source = lax.rem(my_row + n_row - d, n_row)
                span = pl.ds(pl.multiple_of(source * nodes, nodes), nodes)
                prod[...] += jnp.dot(
                    abuf[slot, :, span], panel[span, :], preferred_element_type=F32
                )
                return carry

            lax.fori_loop(0, n_row, add_panel, 0)

        def body(group, carry):
            @pl.when(group < groups)
            def _():
                slot = group % SLOTS
                ahead = group + SLOTS - 1

                @pl.when(ahead < groups)
                def _():
                    for copy in fetch(ahead, ahead % SLOTS):
                        copy.start()

                for copy in fetch(group, slot):
                    copy.wait()
                multiply(group, slot)
                for u in range(GROUP):
                    part, dest = place(group * GROUP + u)
                    at = part * chips + dest
                    first = (GROUP + u) * sub
                    store(sib_out.at[at], prod.at[first : first + sub])
                    sib_copy(at).start()
                for u in range(GROUP):
                    store(own.at[(group % 2) * GROUP + u], prod.at[u * sub : (u + 1) * sub])

            def reduce(u, carry):
                j = (group - 1) * GROUP + u
                part, dest = place(j)
                at = part * chips + dest
                sib_copy(at).wait_recv()
                mine = own.at[((group - 1) % 2) * GROUP + u]

                def forward(copy, arrived, has_up, device):
                    @pl.when(has_up)
                    def _():
                        copy(at, sibling).wait_recv()
                        hop_out[at] = (
                            mine[...] + sib_in[at].astype(F32) + arrived[at].astype(F32)
                        ).astype(BF16)

                    @pl.when(jnp.logical_not(has_up))
                    def _():
                        hop_out[at] = (mine[...] + sib_in[at].astype(F32)).astype(BF16)

                    copy(at, device).start()

                @pl.when(dest > chip)
                def _():
                    forward(right_copy, left_in, has_left, right)

                @pl.when(dest < chip)
                def _():
                    forward(left_copy, right_in, has_right, left)

                @pl.when(dest == chip)
                def _():
                    tot[...] = mine[...] + sib_in[at].astype(F32)

                    @pl.when(has_left)
                    def _():
                        right_copy(at, sibling).wait_recv()
                        tot[...] += left_in[at].astype(F32)

                    @pl.when(has_right)
                    def _():
                        left_copy(at, sibling).wait_recv()
                        tot[...] += right_in[at].astype(F32)

                    finish(part)

                return carry

            @pl.when(group >= 1)
            def _():
                lax.fori_loop(0, GROUP, reduce, 0)

            return carry

        lax.fori_loop(0, groups + 1, body, 0)

        def drain():
            def one(i, carry):
                part, dest = place(i)
                at = part * chips + dest
                sib_copy(at).wait_send()

                @pl.when(dest != chip)
                def _():
                    right_copy(at, sibling).wait_send()

                return carry

            lax.fori_loop(0, steps, one, 0)

        return drain

    def finish1(part):
        for b in range(sub_blocks):
            rows = pl.ds(pl.multiple_of(part * sub + b * blk, blk), blk)
            scale = lax.rsqrt(1.0 + to_col(tot1[sub + b : sub + b + 1, :]))
            scale_ref[rows, :] = jnp.broadcast_to(scale, (blk, blk))
            mean = tot1[b * blk : (b + 1) * blk, :] * scale
            high = mean.astype(BF16)
            low = (mean - high.astype(F32)).astype(BF16)
            before = jnp.dot(high, w1_ref[:, :hid], preferred_element_type=F32)
            before += jnp.dot(low, w1_ref[:, :hid], preferred_element_type=F32)
            before += jnp.dot(x_ref[rows, :], w1_ref[:, hid:], preferred_element_type=F32)
            hidden = jnp.tanh(before).astype(BF16)
            h1_ref[rows, :] = hidden
            mine = pl.ds(pl.multiple_of(my_row * nodes + part * sub + b * blk, blk), blk)
            panel2[mine, :] = jnp.dot(
                hidden, w2_ref[:, :hid], preferred_element_type=F32
            ).astype(BF16)
        share(1, part2, part)

    drain1 = aggregate(
        0, panel1, part1, own1, tot1, sib_out1, sib_in1, hop_out1, left_in1, right_in1, finish1
    )
    for early in range(min(SLOTS - 1, steps // GROUP)):
        for copy in fetch(early, early):
            copy.start()

    def finish2(part):
        for b in range(sub_blocks):
            rows = pl.ds(pl.multiple_of(part * sub + b * blk, blk), blk)
            before = jnp.dot(h1_ref[rows, :], w2_ref[:, hid:], preferred_element_type=F32)
            before += tot2[b * blk : (b + 1) * blk, :] * scale_ref[rows, 0:1] + b2_ref[...]
            panel3[my_row * dev_blocks + part * sub_blocks + b] = jnp.tanh(before).astype(BF16)
        share(2, part3, part)

    drain2 = aggregate(
        1, panel2, part2, own2, tot2, sib_out2, sib_in2, hop_out2, left_in2, right_in2, finish2
    )

    def attr_block(b, carry):
        rows = pl.ds(pl.multiple_of(b * blk, blk), blk)
        rebuilt = jnp.dot(
            panel3[my_row * dev_blocks + b], wa_ref[...], preferred_element_type=F32
        )
        diff = rebuilt + ba_ref[...] - x_ref[rows, :].astype(F32)
        error = jnp.sqrt(jnp.mean(diff * diff, axis=1, keepdims=True) + epsilon)
        attr_ref[rows, :] = jnp.broadcast_to(error, (blk, blk))
        return carry

    lax.fori_loop(0, dev_blocks, attr_block, 0)
    drain1()
    drain2()
    for stage, view in enumerate((part1, part2, part3)):
        shared(stage, view)
    for d in range(1, n_row):
        arrived_from(2, part3, d)

    pair_count = pair_ref.shape[1]

    def decode(b, carry):
        rows = pl.ds(pl.multiple_of(b * blk, blk), blk)
        mine = panel3[my_row * dev_blocks + b]
        total = jnp.zeros((blk, blk), F32)
        for j in range(pair_count):
            logits = lax.dot_general(
                mine,
                panel3[pair_ref[b, j]],
                (((1,), (1,)), ((), ())),
                preferred_element_type=F32,
            ) * hid ** (-0.5)
            diff = jax.nn.sigmoid(logits) - target_ref[rows, j, :].astype(F32)
            total += diff * diff
        mean = jnp.sum(total, axis=1, keepdims=True) * (1.0 / (pair_count * blk))
        score = mix_alpha * attr_ref[rows, :] + (1.0 - mix_alpha) * jnp.sqrt(mean + epsilon)
        out_ref[pl.ds(b, 1), :] = to_row(score)
        return carry

    lax.fori_loop(0, dev_blocks, decode, 0)


def per_device(
    attributes,
    adj_values,
    adj_rows,
    adj_cols,
    adj_count,
    pair_ids,
    struct_target,
    w_first,
    w_rest,
    layer_bias,
    w_attr,
    attr_bias,
):
    n_row = lax.axis_size("row")
    n_col = lax.axis_size("col")
    nodes, f_in = attributes.shape
    blk = adj_values.shape[3]
    hid = w_rest.shape[1]
    row_blocks = n_col * nodes // blk
    col_blocks = n_row * nodes // blk
    dense = dense_tile(
        adj_values[0, 0], adj_rows, adj_cols, adj_count, row_blocks, col_blocks
    )
    sub = nodes // SUBS
    steps = SUBS * (n_col // 2)
    wide = 2 * blk
    vmem = pl.BlockSpec(memory_space=pltpu.VMEM)
    ring1 = pltpu.VMEM((steps, sub + DEG_ROWS, f_in), BF16)
    ring2 = pltpu.VMEM((steps, sub, hid), BF16)
    scores = pl.pallas_call(
        functools.partial(graph_kernel, n_row, n_col),
        out_shape=jax.ShapeDtypeStruct((nodes // blk, blk), F32),
        in_specs=[
            vmem,
            pl.BlockSpec(memory_space=pl.ANY),
            pl.BlockSpec(memory_space=pltpu.SMEM),
        ]
        + [vmem] * 6,
        out_specs=vmem,
        scratch_shapes=[
            pltpu.VMEM((n_row * nodes, f_in + blk), BF16),
            pltpu.VMEM((n_row * nodes, hid), BF16),
            pltpu.VMEM((col_blocks, blk, hid), BF16),
            pltpu.VMEM((SLOTS, 2 * GROUP * sub, col_blocks * blk), BF16),
            pltpu.VMEM((2 * GROUP, sub + DEG_ROWS, f_in), F32),
            pltpu.VMEM((2 * GROUP, sub, hid), F32),
            pltpu.VMEM((sub + DEG_ROWS, f_in), F32),
            pltpu.VMEM((sub, hid), F32),
            pltpu.VMEM((nodes, hid), BF16),
            pltpu.VMEM((nodes, blk), F32),
            pltpu.VMEM((nodes, blk), F32),
        ]
        + [ring1] * 5
        + [ring2] * 5
        + [
            pltpu.SemaphoreType.DMA((SLOTS, 2 * GROUP)),
            pltpu.SemaphoreType.DMA((3, n_row - 1, SUBS)),
            pltpu.SemaphoreType.DMA((3, n_row - 1, SUBS)),
            pltpu.SemaphoreType.DMA((2, steps)),
            pltpu.SemaphoreType.DMA((2, steps)),
            pltpu.SemaphoreType.DMA((2, steps)),
            pltpu.SemaphoreType.DMA((2, steps)),
            pltpu.SemaphoreType.DMA((2, steps)),
            pltpu.VMEM((2 * GROUP * sub, wide), F32),
        ],
        compiler_params=pltpu.CompilerParams(
            collective_id=0, has_side_effects=True, vmem_limit_bytes=56 * 1024 * 1024
        ),
        name="graph_layers",
    )(
        attributes,
        dense,
        pair_ids,
        struct_target,
        w_first,
        w_rest[0],
        layer_bias,
        w_attr,
        attr_bias.reshape(1, -1),
    )
    return scores.reshape(nodes)


def solution(mesh):
    return jax.shard_map(
        per_device,
        mesh=mesh,
        in_specs=(
            P(("row", "col"), None),
            P("row", "col", None, None, None),
            P("row", "col", None),
            P("row", "col", None),
            P("row", "col"),
            P(("row", "col"), None),
            P(("row", "col"), None, None),
            P(),
            P(),
            P(),
            P(),
            P(),
        ),
        out_specs=P(("row", "col")),
        check_vma=False,
    )
```

```python
import functools

import jax
import jax.numpy as jnp
from jax import lax
from jax.experimental import pallas as pl
from jax.experimental.pallas import tpu as pltpu
from jax.sharding import PartitionSpec as P

epsilon = 1e-06
mix_alpha = 0.8
MESH = pl.DeviceIdType.MESH
F32 = jnp.float32
BF16 = jnp.bfloat16
SUBS = 2
LAG = 1
OWN_LAG = 2
DEG_ROWS = 16


def dense_kernel(part_blocks, rows_ref, cols_ref, count_ref, vals_hbm, out_ref, vals_ref, lists, sizes, sem):
    part = pl.program_id(0)
    blk = vals_ref.shape[1]
    load = pltpu.make_async_copy(vals_hbm, vals_ref, sem)

    @pl.when(part == 0)
    def _():
        load.start()
        for q in range(sizes.shape[0]):
            sizes[q] = 0

        def assign(k, carry):
            q = lax.div(rows_ref[k], part_blocks)
            n = sizes[q]
            lists[q, n] = k
            sizes[q] = n + 1
            return carry

        lax.fori_loop(0, count_ref[0], assign, 0)

    out_ref[...] = jnp.zeros_like(out_ref)

    @pl.when(part == 0)
    def _():
        load.wait()

    def add_slot(n, carry):
        k = lists[part, n]
        row = rows_ref[k] - part * part_blocks
        where_r = pl.ds(pl.multiple_of(row * blk, blk), blk)
        where_c = pl.ds(pl.multiple_of(cols_ref[k] * blk, blk), blk)
        out_ref[where_r, where_c] = out_ref[where_r, where_c] + vals_ref[k]
        return carry

    lax.fori_loop(0, sizes[part], add_slot, 0)


def dense_tile(vals, row_ids, col_ids, count, row_blocks, col_blocks):
    cap, blk, _ = vals.shape
    part_blocks = 4
    parts = row_blocks // part_blocks
    grid_spec = pltpu.PrefetchScalarGridSpec(
        num_scalar_prefetch=3,
        grid=(parts,),
        in_specs=[pl.BlockSpec(memory_space=pl.ANY)],
        out_specs=pl.BlockSpec((part_blocks * blk, col_blocks * blk), lambda i, *_: (i, 0)),
        scratch_shapes=[
            pltpu.VMEM((cap, blk, blk), vals.dtype),
            pltpu.SMEM((parts, cap), jnp.int32),
            pltpu.SMEM((parts,), jnp.int32),
            pltpu.SemaphoreType.DMA,
        ],
    )
    dense_bytes = row_blocks * col_blocks * blk * blk * 2
    return pl.pallas_call(
        functools.partial(dense_kernel, part_blocks),
        grid_spec=grid_spec,
        out_shape=jax.ShapeDtypeStruct((row_blocks * blk, col_blocks * blk), vals.dtype),
        compiler_params=pltpu.CompilerParams(vmem_limit_bytes=48 * 1024 * 1024),
        cost_estimate=pl.CostEstimate(
            flops=dense_bytes, bytes_accessed=2 * dense_bytes, transcendentals=0
        ),
        name="dense_tile",
    )(row_ids, col_ids, count, vals)


def graph_kernel(
    n_row,
    n_col,
    *refs,
):
    x_refs, refs = refs[:n_row], refs[n_row:]
    x_ref = x_refs[0]
    (
    a_ref,
    pair_ref,
    target_ref,
    w1_ref,
    w2_ref,
    b2_ref,
    wa_ref,
    ba_ref,
    out_ref,
    panel1,
    panel2,
    panel3,
    abuf,
    own1,
    own2,
    tot1,
    tot2,
    h1_ref,
    scale_ref,
    attr_ref,
    sib_out1,
    sib_in1,
    hop_out1,
    left_in1,
    right_in1,
    sib_out2,
    sib_in2,
    hop_out2,
    left_in2,
    right_in2,
    a_sem,
    g_send,
    g_recv,
    sib_send,
    sib_recv,
    hop_send,
    left_recv,
    right_recv,
    ) = refs
    my_row = lax.axis_index("row")
    my_col = lax.axis_index("col")
    chips = n_col // 2
    chip = my_col // 2
    core = my_col % 2
    nodes, f_in = x_ref.shape
    hid = w2_ref.shape[0]
    blk = panel3.shape[1]
    sub = nodes // SUBS
    sub_blocks = sub // blk
    dev_blocks = nodes // blk
    steps = SUBS * chips

    sibling = (my_row, chip * 2 + 1 - core)
    right = (my_row, my_col + 2)
    left = (my_row, my_col - 2)
    peers = [(lax.rem(my_row + d, n_row), my_col) for d in range(1, n_row)]
    has_left = chip > 0
    has_right = chip < chips - 1

    far = jnp.maximum(chip, chips - 1 - chip)
    near = chips - 1 - far
    toward = jnp.where(2 * chip < chips - 1, 1, -1)

    def place(i):
        lag = min(OWN_LAG, chips - 1)
        first = i < chips - 1
        j = jnp.maximum(i - (chips - 1), 0)
        turn = j // chips
        r = j % chips
        is_own = jnp.logical_not(first) & ((r == lag) | (i == steps - 1))
        part = jnp.where(first, 0, jnp.where(is_own, turn, turn + 1))
        later = jnp.where(is_own, chips - 1, jnp.where(r < lag, r, r - 1))
        s = jnp.where(first, i, later)
        s2 = s - (far - near)
        paired = chip + (near - s2 // 2) * (1 - 2 * (s2 % 2))
        dest = jnp.where(s < far - near, chip + toward * (far - s), paired)
        return part, dest

    eye = lax.broadcasted_iota(jnp.int32, (blk, blk), 0) == lax.broadcasted_iota(
        jnp.int32, (blk, blk), 1
    )

    def to_row(square):
        return jnp.sum(jnp.where(eye, square, 0.0), axis=0, keepdims=True)

    def to_col(row):
        return jnp.sum(jnp.where(eye, jnp.broadcast_to(row, (blk, blk)), 0.0), axis=1, keepdims=True)

    def fetch(i, slot):
        part, dest = place(i)
        copies = []
        for which in range(2):
            pick = core if which == 0 else 1 - core
            start = pl.multiple_of((dest * 2 + pick) * nodes + part * sub, sub)
            copies.append(
                pltpu.make_async_copy(
                    a_ref.at[pl.ds(start, sub), :],
                    abuf.at[slot, pl.ds(which * sub, sub), :],
                    a_sem.at[slot, which],
                )
            )
        return copies

    def remote(src, dst, send, recv, device):
        return pltpu.make_async_remote_copy(
            src_ref=src,
            dst_ref=dst,
            send_sem=send,
            recv_sem=recv,
            device_id=device,
            device_id_type=MESH,
        )

    for copy in fetch(0, 0):
        copy.start()

    barrier = pltpu.get_barrier_semaphore()
    for device in [sibling] + peers:
        pl.semaphore_signal(barrier, inc=1, device_id=device, device_id_type=MESH)

    @pl.when(has_left)
    def _():
        pl.semaphore_signal(barrier, inc=1, device_id=left, device_id_type=MESH)

    @pl.when(has_right)
    def _():
        pl.semaphore_signal(barrier, inc=1, device_id=right, device_id_type=MESH)

    panel1[:, f_in:] = jnp.ones((n_row * nodes, panel1.shape[1] - f_in), BF16)
    for d in range(n_row):
        source = lax.rem(my_row + n_row - d, n_row)
        panel1[pl.ds(pl.multiple_of(source * nodes, nodes), nodes), :f_in] = x_refs[d][...]

    pl.semaphore_wait(barrier, n_row + jnp.minimum(chip, 1) + jnp.minimum(chips - 1 - chip, 1))

    def part2(row, part):
        return panel2.at[pl.ds(pl.multiple_of(row * nodes + part * sub, sub), sub), :]

    def part3(row, part):
        return panel3.at[pl.ds(row * dev_blocks + part * sub_blocks, sub_blocks)]

    def share(stage, view, part):
        for d in range(1, n_row):
            remote(
                view(my_row, part),
                view(my_row, part),
                g_send.at[stage, d - 1, part],
                g_recv.at[stage, d - 1, part],
                peers[d - 1],
            ).start()

    def gathered(stage, view, sent):
        for part in range(SUBS):
            for d in range(1, n_row):
                source = lax.rem(my_row + n_row - d, n_row)
                copy = remote(
                    view(my_row if sent else source, part),
                    view(my_row if sent else source, part),
                    g_send.at[stage, d - 1, part],
                    g_recv.at[stage, d - 1, part],
                    peers[d - 1],
                )
                if sent:
                    copy.wait_send()
                else:
                    copy.wait_recv()

    def aggregate(layer, panel, own, tot, sib_out, sib_in, hop_out, left_in, right_in, finish):
        def store(dst, value):
            if layer == 1:
                dst[...] = value.astype(dst.dtype)
                return
            dst[:sub, :] = value[:, :f_in].astype(dst.dtype)
            lane = lax.broadcasted_iota(jnp.int32, (DEG_ROWS, blk), 0)
            degree = jnp.zeros((DEG_ROWS, blk), F32)
            for b in range(sub_blocks):
                row = to_row(value[b * blk : (b + 1) * blk, f_in : f_in + blk])
                degree = jnp.where(lane == b, jnp.broadcast_to(row, (DEG_ROWS, blk)), degree)
            dst[sub:, :] = degree.astype(dst.dtype)

        def sib_copy(at):
            return remote(
                sib_out.at[at], sib_in.at[at], sib_send.at[layer, at], sib_recv.at[layer, at], sibling
            )

        def right_copy(at, device):
            return remote(
                hop_out.at[at], left_in.at[at], hop_send.at[layer, at], left_recv.at[layer, at], device
            )

        def left_copy(at, device):
            return remote(
                hop_out.at[at], right_in.at[at], hop_send.at[layer, at], right_recv.at[layer, at], device
            )

        def body(i, carry):
            @pl.when(i < steps)
            def _():
                slot = i % 2

                @pl.when(i + 1 < steps)
                def _():
                    for copy in fetch(i + 1, (i + 1) % 2):
                        copy.start()

                for copy in fetch(i, slot):
                    copy.wait()
                part, dest = place(i)
                at = part * chips + dest
                total = jnp.dot(abuf[slot], panel[...], preferred_element_type=F32)
                store(sib_out.at[at], total[sub:])
                sib_copy(at).start()
                store(own.at[i % (LAG + 1)], total[:sub])

            @pl.when(i >= LAG)
            def _():
                j = i - LAG
                part, dest = place(j)
                at = part * chips + dest
                sib_copy(at).wait_recv()
                mine = own.at[j % (LAG + 1)]

                def forward(copy, arrived, has_up, device):
                    @pl.when(has_up)
                    def _():
                        copy(at, sibling).wait_recv()
                        hop_out[at] = (
                            mine[...] + sib_in[at].astype(F32) + arrived[at].astype(F32)
                        ).astype(BF16)

                    @pl.when(jnp.logical_not(has_up))
                    def _():
                        hop_out[at] = (mine[...] + sib_in[at].astype(F32)).astype(BF16)

                    copy(at, device).start()

                @pl.when(dest > chip)
                def _():
                    forward(right_copy, left_in, has_left, right)

                @pl.when(dest < chip)
                def _():
                    forward(left_copy, right_in, has_right, left)

                @pl.when(dest == chip)
                def _():
                    tot[...] = mine[...] + sib_in[at].astype(F32)

                    @pl.when(has_left)
                    def _():
                        right_copy(at, sibling).wait_recv()
                        tot[...] += left_in[at].astype(F32)

                    @pl.when(has_right)
                    def _():
                        left_copy(at, sibling).wait_recv()
                        tot[...] += right_in[at].astype(F32)

                    finish(part)

            return carry

        lax.fori_loop(0, steps + LAG, body, 0)

        def drain():
            def one(i, carry):
                part, dest = place(i)
                at = part * chips + dest
                sib_copy(at).wait_send()

                @pl.when(dest != chip)
                def _():
                    right_copy(at, sibling).wait_send()

                return carry

            lax.fori_loop(0, steps, one, 0)

        return drain

    def finish1(part):
        for b in range(sub_blocks):
            rows = pl.ds(pl.multiple_of(part * sub + b * blk, blk), blk)
            scale = lax.rsqrt(1.0 + to_col(tot1[sub + b : sub + b + 1, :]))
            scale_ref[rows, :] = jnp.broadcast_to(scale, (blk, blk))
            mean = tot1[b * blk : (b + 1) * blk, :] * scale
            high = mean.astype(BF16)
            low = (mean - high.astype(F32)).astype(BF16)
            before = jnp.dot(high, w1_ref[:, :hid], preferred_element_type=F32)
            before += jnp.dot(low, w1_ref[:, :hid], preferred_element_type=F32)
            before += jnp.dot(x_ref[rows, :], w1_ref[:, hid:], preferred_element_type=F32)
            hidden = jnp.tanh(before).astype(BF16)
            h1_ref[rows, :] = hidden
            mine = pl.ds(pl.multiple_of(my_row * nodes + part * sub + b * blk, blk), blk)
            panel2[mine, :] = jnp.dot(
                hidden, w2_ref[:, :hid], preferred_element_type=F32
            ).astype(BF16)
        share(0, part2, part)

    drain1 = aggregate(
        0, panel1, own1, tot1, sib_out1, sib_in1, hop_out1, left_in1, right_in1, finish1
    )
    for copy in fetch(0, 0):
        copy.start()
    gathered(0, part2, False)

    def finish2(part):
        for b in range(sub_blocks):
            rows = pl.ds(pl.multiple_of(part * sub + b * blk, blk), blk)
            before = jnp.dot(h1_ref[rows, :], w2_ref[:, hid:], preferred_element_type=F32)
            before += tot2[b * blk : (b + 1) * blk, :] * scale_ref[rows, 0:1] + b2_ref[...]
            panel3[my_row * dev_blocks + part * sub_blocks + b] = jnp.tanh(before).astype(BF16)
        share(1, part3, part)

    drain2 = aggregate(
        1, panel2, own2, tot2, sib_out2, sib_in2, hop_out2, left_in2, right_in2, finish2
    )

    def attr_block(b, carry):
        rows = pl.ds(pl.multiple_of(b * blk, blk), blk)
        rebuilt = jnp.dot(
            panel3[my_row * dev_blocks + b], wa_ref[...], preferred_element_type=F32
        )
        diff = rebuilt + ba_ref[...] - x_ref[rows, :].astype(F32)
        error = jnp.sqrt(jnp.mean(diff * diff, axis=1, keepdims=True) + epsilon)
        attr_ref[rows, :] = jnp.broadcast_to(error, (blk, blk))
        return carry

    lax.fori_loop(0, dev_blocks, attr_block, 0)
    drain1()
    drain2()
    for stage, view in enumerate((part2, part3)):
        gathered(stage, view, True)
    gathered(1, part3, False)

    pair_count = pair_ref.shape[1]

    def decode(b, carry):
        rows = pl.ds(pl.multiple_of(b * blk, blk), blk)
        mine = panel3[my_row * dev_blocks + b]
        total = jnp.zeros((blk, blk), F32)
        for j in range(pair_count):
            logits = lax.dot_general(
                mine,
                panel3[pair_ref[b, j]],
                (((1,), (1,)), ((), ())),
                preferred_element_type=F32,
            ) * hid ** (-0.5)
            diff = jax.nn.sigmoid(logits) - target_ref[rows, j, :].astype(F32)
            total += diff * diff
        mean = jnp.sum(total, axis=1, keepdims=True) * (1.0 / (pair_count * blk))
        score = mix_alpha * attr_ref[rows, :] + (1.0 - mix_alpha) * jnp.sqrt(mean + epsilon)
        out_ref[pl.ds(b, 1), :] = to_row(score)
        return carry

    lax.fori_loop(0, dev_blocks, decode, 0)


def per_device(
    attributes,
    adj_values,
    adj_rows,
    adj_cols,
    adj_count,
    pair_ids,
    struct_target,
    w_first,
    w_rest,
    layer_bias,
    w_attr,
    attr_bias,
):
    n_row = lax.axis_size("row")
    n_col = lax.axis_size("col")
    nodes, f_in = attributes.shape
    blk = adj_values.shape[3]
    hid = w_rest.shape[1]
    row_blocks = n_col * nodes // blk
    col_blocks = n_row * nodes // blk
    others = [
        lax.ppermute(attributes, "row", [(r, (r + d) % n_row) for r in range(n_row)])
        for d in range(1, n_row)
    ]
    dense = dense_tile(
        adj_values[0, 0], adj_rows[0, 0], adj_cols[0, 0], adj_count[0], row_blocks, col_blocks
    )
    sub = nodes // SUBS
    steps = SUBS * (n_col // 2)
    wide = 2 * blk
    vmem = pl.BlockSpec(memory_space=pltpu.VMEM)
    ring1 = pltpu.VMEM((steps, sub + DEG_ROWS, f_in), BF16)
    ring2 = pltpu.VMEM((steps, sub, hid), BF16)
    scores = pl.pallas_call(
        functools.partial(graph_kernel, n_row, n_col),
        out_shape=jax.ShapeDtypeStruct((nodes // blk, blk), F32),
        in_specs=[vmem] * n_row
        + [
            pl.BlockSpec(memory_space=pl.ANY),
            pl.BlockSpec(memory_space=pltpu.SMEM),
        ]
        + [vmem] * 6,
        out_specs=vmem,
        scratch_shapes=[
            pltpu.VMEM((n_row * nodes, f_in + blk), BF16),
            pltpu.VMEM((n_row * nodes, hid), BF16),
            pltpu.VMEM((col_blocks, blk, hid), BF16),
            pltpu.VMEM((2, 2 * sub, col_blocks * blk), BF16),
            pltpu.VMEM((LAG + 1, sub + DEG_ROWS, f_in), F32),
            pltpu.VMEM((LAG + 1, sub, hid), F32),
            pltpu.VMEM((sub + DEG_ROWS, f_in), F32),
            pltpu.VMEM((sub, hid), F32),
            pltpu.VMEM((nodes, hid), BF16),
            pltpu.VMEM((nodes, blk), F32),
            pltpu.VMEM((nodes, blk), F32),
        ]
        + [ring1] * 5
        + [ring2] * 5
        + [
            pltpu.SemaphoreType.DMA((2, 2)),
            pltpu.SemaphoreType.DMA((2, n_row - 1, SUBS)),
            pltpu.SemaphoreType.DMA((2, n_row - 1, SUBS)),
            pltpu.SemaphoreType.DMA((2, steps)),
            pltpu.SemaphoreType.DMA((2, steps)),
            pltpu.SemaphoreType.DMA((2, steps)),
            pltpu.SemaphoreType.DMA((2, steps)),
            pltpu.SemaphoreType.DMA((2, steps)),
        ],
        compiler_params=pltpu.CompilerParams(
            collective_id=0, has_side_effects=True, vmem_limit_bytes=56 * 1024 * 1024
        ),
        name="graph_layers",
    )(
        attributes,
        *others,
        dense,
        pair_ids,
        struct_target,
        w_first,
        w_rest[0],
        layer_bias,
        w_attr,
        attr_bias.reshape(1, -1),
    )
    return scores.reshape(nodes)


def solution(mesh):
    return jax.shard_map(
        per_device,
        mesh=mesh,
        in_specs=(
            P(("row", "col"), None),
            P("row", "col", None, None, None),
            P("row", "col", None),
            P("row", "col", None),
            P("row", "col"),
            P(("row", "col"), None),
            P(("row", "col"), None, None),
            P(),
            P(),
            P(),
            P(),
            P(),
        ),
        out_specs=P(("row", "col")),
        check_vma=False,
    )
```
